32 devices in a mesh: grp: 2 (over core), tx: 4 (over y, x), ty: 4 (over z).
Axes of the slice: x: 2, y: 2, z: 4, core: 2. Of those that a mesh axis runs over, the one named last changes fastest.
Arguments:
- endpoints: float32 [2, 5, 16, 32, 512], P('grp', None, None, 'tx', 'ty'), may hold values from -4 to 5, as said below
Outputs:
- adjoints: float32 [2, 5, 16, 32, 512], P('grp', None, None, 'tx', 'ty')
- forward_states: float32 [2, 5, 16, 32, 512], P('grp', None, None, 'tx', 'ty')
The draws below stay inside these ranges and needn't reach their ends.
Inputs may be any that keep to these rules, and one draw needn't show every extreme that they name: `endpoints`: in entry 0 the density lies in 1 to 2, each velocity component (momentum over density) in -0.5 to 0.5 and the pressure 0.4 (E - |m|^2 / (2 density)) in 0.5 to 1.5; entry 1 is a cotangent within -4 to 4.
All inputs are finite; a program needn't handle non-finite values.
Results may differ from the reference program's by a relative error of at most 0.00002.
Values sent between devices are 32-bit elements; how exact they have to be, the bound alone decides.
No kernel may reach another device: no remote copies, remote signals or barrier semaphores. Data moves between devices by JAX's collectives and lax.ppermute only.
A program may use at most 64 MiB of HBM per device.

```python
import jax
import jax.numpy as jnp

NZ = 16
NX = 32
NY = 512


gas_gamma = 1.4


def draw_endpoints(key, part):
    keys = jax.random.split(jax.random.fold_in(key, 17), 5)
    grid_shape = (NZ, NX, NY)
    density = jax.random.uniform(keys[0], grid_shape, jnp.float32, 1.0, 2.0)
    cotangent = jnp.clip(jax.random.normal(keys[3], (5,) + grid_shape, jnp.float32), -4.0, 4.0)
    velocity = jax.random.uniform(keys[1], (3,) + grid_shape, jnp.float32, -0.5, 0.5)
    pressure = jax.random.uniform(keys[2], grid_shape, jnp.float32, 0.5, 1.5)
    momentum = density[None] * velocity
    energy = pressure / (gas_gamma - 1.0) + 0.5 * density * jnp.sum(velocity * velocity, axis=0)
    fields = jnp.concatenate([density[None], momentum, energy[None]], axis=0)
    return jnp.stack([fields, cotangent])


def setup_inputs(seed: int = 0) -> dict:
    arg_keys = jax.random.split(jax.random.key(seed), 2)
    return {
        "endpoints": draw_endpoints(jax.random.fold_in(arg_keys[1], 71), 0),
    }


gas_gamma = 1.4
time_step = 0.05
viscosity = 0.1
directions = ((1, 2), (2, 3), (3, 1))

def euler_flux(fields, component):
    density = fields[0]
    inverse = 1.0 / density
    kinetic = 0.5 * inverse * (fields[1] * fields[1] + fields[2] * fields[2] + fields[3] * fields[3])
    pressure = (gas_gamma - 1.0) * (fields[4] - kinetic)
    velocity = fields[component] * inverse
    components = [fields[component], fields[1] * velocity, fields[2] * velocity, fields[3] * velocity, (fields[4] + pressure) * velocity]
    components[component] = components[component] + pressure
    return jnp.stack(components)

def rate_field(fields):
    tendency = jnp.zeros_like(fields)
    for component, spatial in directions:
        fluxes = euler_flux(fields, component)
        tendency = tendency - 0.5 * (jnp.roll(fluxes, -1, spatial) - jnp.roll(fluxes, 1, spatial))
        tendency = tendency + viscosity * (jnp.roll(fields, -1, spatial) + jnp.roll(fields, 1, spatial) - 2.0 * fields)
    return tendency

def heun_step(fields):
    first_rate = rate_field(fields)
    section_state = fields + time_step * first_rate
    return fields + 0.5 * time_step * (first_rate + rate_field(section_state))

def reference(endpoints):
    initial = endpoints[0]
    final_cot = endpoints[1]
    midway = heun_step(initial)
    ending = heun_step(midway)
    outputs, pullback = jax.vjp(heun_step, midway)
    middle_cot, = pullback(final_cot)
    outputs, pullback = jax.vjp(heun_step, initial)
    start_cot, = pullback(middle_cot)
    return (jnp.stack([start_cot, middle_cot]), jnp.stack([midway, ending]))
```

```python
import jax
import jax.numpy as jnp
from jax import lax
from jax.experimental import pallas as pl
from jax.experimental.pallas import tpu as pltpu
from jax.sharding import PartitionSpec as P


NF = 5
WS = 6
WC = 4
ROWS = 8
HALF = 64
LANES = 128
TOTAL = ROWS + 2 * WS
FK = [(f, k) for f in range(NF) for k in range(2)]
VMEM_LIMIT = 32 * 2**20
UNROLL = 2


def lanes():
    lane = lax.broadcasted_iota(jnp.int32, (8, LANES), 1)
    core = lax.axis_index("grp")
    return lane, core, (lane + HALF * core) & (LANES - 1)


def turn(x, shift):
    return pltpu.roll(x, shift % LANES, 1)


def pack_kernel(own_ref, got_ref, t0, t1, up0, down0, up1, down1, side):
    lane, core, q = lanes()
    mine = q < HALF
    first = core == 0
    for f, k in FK:
        state, cot = [], []
        for r in range(ROWS):
            rows = pl.ds(f * 16 * ROWS + k * ROWS + r, 8, stride=2 * ROWS)
            a, b = own_ref[rows, :], got_ref[rows, :]
            state.append(jnp.where(first, a, b))
            cot.append(jnp.where(first, b, a))
            t0[r, f, k] = state[r]
            t1[r, f, k] = cot[r]
        for src, width, up, down in ((state, WS, up0, down0), (cot, WC, up1, down1)):
            n = width // 2
            for j in range(n):
                up[j, f, k] = jnp.where(
                    mine, src[ROWS - width + j], turn(src[ROWS - n + j], HALF)
                )
                down[j, f, k] = jnp.where(mine, src[j], turn(src[n + j], HALF))
        acc = jnp.zeros((8, LANES), jnp.float32)
        for src, width, base in ((state, WS, 0), (cot, WC, ROWS * WS)):
            for r in range(ROWS):
                at = base + width * r
                moved = pltpu.roll(src[r], at + width * core, 1)
                acc = jnp.where((lane >= at) & (lane < at + width), moved, acc)
        side[f, k] = acc


def beside(side, f, k, r, width, base, lane, core, tile):
    shift = LANES - width - base - width * r + width * core
    shift = jnp.where(shift >= LANES, shift - LANES, shift)
    moved = pltpu.roll(side[f, k], shift, 1)
    outer = ((lane + width * (1 - core)) & (LANES - 1)) < width
    return jnp.where(outer, moved, tile)


def corner_kernel(t0, t1, side, up, down):
    lane, core, q = lanes()
    for f, k in FK:
        tight = []
        for src, width, base in ((t0, WS, 0), (t1, WC, ROWS * WS)):
            rows = []
            for r in range(ROWS):
                full = beside(side, f, k, r, width, base, lane, core, src[r, f, k])
                gap = LANES - HALF - 2 * width
                rows.append(jnp.where(q >= HALF + width, turn(full, -gap), full))
            tight.append(rows)
        for out, lift in ((up, True), (down, False)):
            acc = jnp.zeros((8, LANES), jnp.float32)
            for rows, width, base in ((tight[0], WS, 0), (tight[1], WC, 2 * WS * WS)):
                for j in range(width):
                    at = base + 2 * width * j
                    moved = turn(rows[ROWS - width + j if lift else j], at - HALF)
                    acc = jnp.where((q >= at) & (q < at + 2 * width), moved, acc)
            out[f, k] = acc


def halo_row(packed, corner, f, k, j, width, base, q):
    n = width // 2
    row = packed[j % n, f, k]
    if j >= n:
        row = turn(row, HALF)
    at = base + 2 * width * j
    c = corner[f, k]
    row = jnp.where((q >= HALF) & (q < HALF + width), turn(c, HALF - at), row)
    return jnp.where(q >= LANES - width, turn(c, LANES - 2 * width - at), row)


def assemble(dst, offset, tile, side, low, high, clow, chigh, width, sbase, cbase):
    lane, core, q = lanes()
    for f, k in FK:
        for r in range(ROWS):
            dst[offset + width + r, f, k] = beside(
                side, f, k, r, width, sbase, lane, core, tile[r, f, k]
            )
        for j in range(width):
            dst[offset + j, f, k] = halo_row(low, clow, f, k, j, width, cbase, q)
            dst[offset + width + ROWS + j, f, k] = halo_row(
                high, chigh, f, k, j, width, cbase, q
            )


def load(ref, r):
    return [[ref[r, f, k] for f in range(NF)] for k in range(2)]


def invert(x):
    r = pl.reciprocal(x, approx=True)
    r = r * (2.0 - x * r)
    return r * (2.0 - x * r)


def fluxes(v):
    rho, m1, m2, m3, en = v
    inv = invert(rho)
    v1, v2, v3 = m1 * inv, m2 * inv, m3 * inv
    a, b, c = m1 * v1, m2 * v2, m3 * v3
    p = 0.4 * (en - 0.5 * (a + b + c))
    h = en + p
    m12, m13, m23 = m1 * v2, m1 * v3, m2 * v3
    return (
        (m1, a + p, m12, m13, h * v1),
        (m2, m12, b + p, m23, h * v2),
        (m3, m13, m23, c + p, h * v3),
    )


def pieces(v, want):
    prev = [[None] * 2 for _ in range(NF)]
    after = [[None] * 2 for _ in range(NF)]
    here = [[None] * 2 for _ in range(NF)]
    fl = [fluxes(v[k]) for k in range(2)]
    for f in range(NF):
        s = [0.2 * v[k][f] for k in range(2)]
        if "prev" in want:
            prev[f] = [s[k] - fl[k][0][f] for k in range(2)]
        if "after" in want:
            after[f] = [s[k] + fl[k][0][f] for k in range(2)]
        if "here" in want:
            ym = [s[k] - fl[k][1][f] for k in range(2)]
            yp = [s[k] + fl[k][1][f] for k in range(2)]
            zm = [s[k] - fl[k][2][f] for k in range(2)]
            zp = [s[k] + fl[k][2][f] for k in range(2)]
            zc = [
                zm[1] + pltpu.roll(zp[1], 1, 0),
                pltpu.roll(zm[0], 7, 0) + zp[0],
            ]
            here[f] = [
                (turn(ym[k], -1) + turn(yp[k], 1)) + (zc[k] - 1.2 * v[k][f])
                for k in range(2)
            ]
    return prev, after, here


def flat(x):
    return tuple(x[f][k] for f, k in FK)


def rate_pass(src, lo, hi, emit):
    _, after, _ = pieces(load(src, lo), ("after",))
    prev_after = flat(after)
    _, after, here = pieces(load(src, lo + 1), ("after", "here"))
    pend = tuple(a + b for a, b in zip(flat(here), prev_after))

    def body(r, carry):
        pend, prev_after = carry
        prev, after, here = pieces(load(src, r), ("prev", "after", "here"))
        emit(r - 1, [a + b for a, b in zip(pend, flat(prev))])
        return tuple(a + b for a, b in zip(flat(here), prev_after)), flat(after)

    pend, _ = lax.fori_loop(lo + 2, hi - 1, body, (pend, flat(after)), unroll=UNROLL)
    prev, _, _ = pieces(load(src, hi - 1), ("prev",))
    emit(hi - 2, [a + b for a, b in zip(pend, flat(prev))])


def forward_kernel(tile, side, low, high, clow, chigh, s0, u1, s1, u2, u0):
    assemble(u0, 0, tile, side, low, high, clow, chigh, WS, 0, 0)

    def section(base, dst):
        def emit(r, rate):
            for (f, k), x in zip(FK, rate):
                dst[r, f, k] = base[r, f, k] + 0.025 * x

        return emit

    def advance(base, sec, dst, shift):
        def emit(r, rate):
            for (f, k), x in zip(FK, rate):
                mean = 0.5 * (base[r, f, k] + sec[r, f, k])
                dst[r - shift, f, k] = mean + 0.0125 * x

        return emit

    rate_pass(u0, 0, TOTAL, section(u0, s0))
    rate_pass(s0, 1, TOTAL - 1, advance(u0, s0, u1, 0))
    rate_pass(u1, 2, TOTAL - 2, section(u1, s1))
    rate_pass(s1, WS - 1, WS + ROWS + 1, advance(u1, s1, u2, WS))


def pulled(state, w, r, emit, sr=None):
    v = load(state, r if sr is None else sr)
    wm, wc, wp = load(w, r - 1), load(w, r), load(w, r + 1)
    for k in range(2):
        rho, m1, m2, m3, en = v[k]
        inv = invert(rho)
        v1, v2, v3 = m1 * inv, m2 * inv, m3 * inv
        kin = 0.5 * (v1 * v1 + v2 * v2 + v3 * v3)
        p = 0.4 * (en - rho * kin)
        h = (en + p) * inv
        d1, d2, d3, around = [], [], [], []
        for f in range(NF):
            left, right = turn(wc[k][f], 1), turn(wc[k][f], -1)
            if k == 0:
                below, above = pltpu.roll(wc[1][f], 1, 0), wc[1][f]
            else:
                below, above = wc[0][f], pltpu.roll(wc[0][f], 7, 0)
            d1.append(wp[k][f] - wm[k][f])
            d2.append(right - left)
            d3.append(above - below)
            around.append(
                ((wp[k][f] + wm[k][f]) + (right + left)) + (above + below)
            )
        a = [(m1 * d1[f] + m2 * d2[f] + m3 * d3[f]) * (1.0 if f == 0 else inv) for f in range(NF)]
        b1, b2, b3 = [
            d[0] + v1 * d[1] + v2 * d[2] + v3 * d[3] + h * d[4] for d in (d1, d2, d3)
        ]
        pc = 0.4 * (d1[1] + d2[2] + d3[3] + a[4])
        out = [
            pc * kin - (a[1] * v1 + a[2] * v2 + a[3] * v3 + a[4] * h),
            b1 + a[1] - pc * v1,
            b2 + a[2] - pc * v2,
            b3 + a[3] - pc * v3,
            a[4] + pc,
        ]
        for f in range(NF):
            emit(f, k, out[f] + (0.2 * around[f] - 1.2 * wc[k][f]), wc[k][f])


def adjoint_kernel(
    tile0, tile1, side, low, high, clow, chigh, s0, u1, s1, u2,
    keep_a, keep_s, send, lam, cot, wgt, lam1,
):
    assemble(lam, WS - WC, tile1, side, low, high, clow, chigh, WC, ROWS * WS, 2 * WS * WS)
    lane, core, q = lanes()
    first = core == 0
    mine = q < HALF

    def section(state, lam, lo, hi):
        def body(r, _):
            def emit(f, k, x, w):
                c = 0.0125 * x
                cot[r, f, k] = c
                wgt[r, f, k] = 0.0125 * w + 0.025 * c

            pulled(state, lam, r, emit)
            return 0

        lax.fori_loop(lo, hi, body, 0, unroll=UNROLL)

    section(s1, lam, 3, TOTAL - 3)

    def first_body(r, _):
        def emit(f, k, x, w):
            lam1[r, f, k] = lam[r, f, k] + cot[r, f, k] + x

        pulled(u1, wgt, r, emit)
        return 0

    lax.fori_loop(4, TOTAL - 4, first_body, 0, unroll=UNROLL)
    section(s0, lam1, 5, TOTAL - 5)

    def last_body(r, _):
        i = r - WS

        def emit(f, k, x, w):
            before = lam1[r, f, k]
            start = before + cot[r, f, k] + x
            mid, end = u1[r, f, k], u2[i, f, k]
            keep_a[i, f, k] = jnp.where(first, start, before)
            keep_s[i, f, k] = jnp.where(first, mid, end)
            away_a = jnp.where(first, before, start)
            away_s = jnp.where(first, end, mid)
            send[i, f, k] = jnp.where(mine, away_a, turn(away_s, HALF))

        pulled(tile0, wgt, r, emit, sr=i)
        return 0

    lax.fori_loop(WS, WS + ROWS, last_body, 0, unroll=UNROLL)


def merge_kernel(keep_a, keep_s, got, out_a, out_s):
    lane, core, q = lanes()
    mine = q < HALF
    for f, k in FK:
        for r in range(ROWS):
            rows = pl.ds(f * 16 * ROWS + k * ROWS + r, 8, stride=2 * ROWS)
            other = got[r, f, k]
            out_a[rows, :] = jnp.where(mine, keep_a[r, f, k], other)
            out_s[rows, :] = jnp.where(mine, keep_s[r, f, k], turn(other, HALF))


def call(kernel, outs, scratch, *args, flops=0):
    shapes = [jax.ShapeDtypeStruct(s, jnp.float32) for s in outs]
    size = 4 * sum(a.size for a in args)
    return pl.pallas_call(
        kernel,
        out_shape=shapes,
        scratch_shapes=[pltpu.VMEM(s, jnp.float32) for s in scratch],
        compiler_params=pltpu.CompilerParams(vmem_limit_bytes=VMEM_LIMIT),
        cost_estimate=pl.CostEstimate(flops=flops, bytes_accessed=size, transcendentals=0),
    )(*args)


def rows_of(n):
    return (n, NF, 2, 8, LANES)


def ring(count, step):
    return [(i, (i + step) % count) for i in range(count)]


def shards(endpoints):
    shape = endpoints.shape
    tx, ty = lax.axis_size("tx"), lax.axis_size("ty")
    own = endpoints.reshape(-1, LANES)
    swap = [(0, 1), (1, 0)]
    got = lax.ppermute(own, "grp", swap)
    block = (NF, 2, 8, LANES)
    t0, t1, up0, down0, up1, down1, side = call(
        pack_kernel,
        [rows_of(ROWS), rows_of(ROWS), rows_of(WS // 2), rows_of(WS // 2),
         rows_of(WC // 2), rows_of(WC // 2), block],
        [],
        own, got,
    )
    pairs = [(i, ty + (i - 1) % ty) for i in range(ty)]
    pairs += [(b, a) for a, b in pairs]
    side = lax.ppermute(side, ("grp", "ty"), pairs)
    low0 = lax.ppermute(up0, "tx", ring(tx, 1))
    high0 = lax.ppermute(down0, "tx", ring(tx, -1))
    cup, cdown = call(corner_kernel, [block, block], [], t0, t1, side)
    clow = lax.ppermute(cup, "tx", ring(tx, 1))
    chigh = lax.ppermute(cdown, "tx", ring(tx, -1))
    low1 = lax.ppermute(up1, "tx", ring(tx, 1))
    high1 = lax.ppermute(down1, "tx", ring(tx, -1))
    full = rows_of(TOTAL)
    s0, u1, s1, u2 = call(
        forward_kernel, [full, full, full, rows_of(ROWS)], [full],
        t0, side, low0, high0, clow, chigh, flops=10**7,
    )
    keep_a, keep_s, send = call(
        adjoint_kernel, [rows_of(ROWS)] * 3, [full] * 4,
        t0, t1, side, low1, high1, clow, chigh, s0, u1, s1, u2, flops=10**7,
    )
    other = lax.ppermute(send, "grp", swap)
    adjoints, states = call(
        merge_kernel, [own.shape, own.shape], [], keep_a, keep_s, other
    )
    return adjoints.reshape(shape), states.reshape(shape)


def solution(mesh):
    placed = P("grp", None, None, "tx", "ty")
    return jax.shard_map(
        shards, mesh=mesh, in_specs=(placed,), out_specs=(placed, placed), check_vma=False
    )
```

```python
import jax
import jax.numpy as jnp
from jax import lax
from jax.experimental import pallas as pl
from jax.experimental.pallas import tpu as pltpu
from jax.sharding import PartitionSpec as P


NF = 5
WS = 6
WC = 4
ROWS = 8
HALF = 64
LANES = 128
TOTAL = ROWS + 2 * WS
FK = [(f, k) for f in range(NF) for k in range(2)]
VMEM_LIMIT = 32 * 2**20
UNROLL = 4
CORNER = WS * (WS - 1) // 2 + WC * (WC - 1) // 2


def lanes():
    lane = lax.broadcasted_iota(jnp.int32, (8, LANES), 1)
    core = lax.axis_index("grp")
    return lane, core


def owned(lane, core):
    return ((lane + HALF * core) & (LANES - 1)) < HALF


def turn(x, shift):
    if isinstance(shift, int):
        shift %= LANES
    else:
        shift &= LANES - 1
    return pltpu.roll(x, shift, 1)


def triangle(width, base):
    return [(w, base + w * (w - 1) // 2) for w in reversed(range(width))]


def corner(which):
    return triangle(WS, 0) if which == 0 else triangle(WC, WS * (WS - 1) // 2)


def tile_lane(which, r):
    if which == 0:
        return CORNER + WS * r if r < 5 else HALF + CORNER + WS * (r - 5)
    if r < 3:
        return CORNER + 5 * WS + WC * r
    return HALF + CORNER + 3 * WS + WC * (r - 3)


def own_kernel(own, rows_out):
    for f, k in FK:
        for r in range(ROWS):
            rows = pl.ds(f * 16 * ROWS + k * ROWS + r, 8, stride=2 * ROWS)
            rows_out[r, f, k] = own[rows, :]


def pack_rows(tile, outs, width, lane, core):
    mine = owned(lane, core)
    n = width // 2
    for out, start in zip(outs, (ROWS - width, 0)):
        for j in range(n):
            dst, i = out(j)
            for f, k in FK:
                pair = turn(tile[start + n + j, f, k], HALF)
                dst[i + 2 * f + k] = jnp.where(mine, tile[start + j, f, k], pair)


def pack_kernel(own, got, t0, t1, first_up, first_down, rest_up, rest_down, side):
    lane, core = lanes()
    first = core == 0
    zero = jnp.zeros((8, LANES), jnp.float32)
    sides = [zero for _ in FK]
    edges = [[zero] * NF for _ in range(2)]
    for r in range(ROWS):
        rows = [[], []]
        for f, k in FK:
            at = pl.ds(f * 16 * ROWS + k * ROWS + r, 8, stride=2 * ROWS)
            a, b = own[r, f, k], got[at, :]
            rows[0].append(jnp.where(first, a, b))
            rows[1].append(jnp.where(first, b, a))
            t0[r, f, k] = rows[0][-1]
            t1[r, f, k] = rows[1][-1]
        for which, width in ((0, WS), (1, WC)):
            at = tile_lane(which, r)
            for k in range(2):
                place = (lane - 32 * k) & (LANES - 1)
                mask = (place >= at) & (place < at + width)
                for f in range(NF):
                    i = 2 * f + k
                    moved = turn(rows[which][i], at + 32 * k + width * core)
                    sides[i] = jnp.where(mask, moved, sides[i])
            for d, away in ((0, ROWS - 1 - r), (1, r)):
                if away >= width:
                    continue
                w, at2 = corner(which)[away]
                if w == 0:
                    continue
                for k in range(2):
                    place = (lane - 32 * k) & (HALF - 1)
                    mask = (place >= at2) & (place < at2 + w)
                    for f in range(NF):
                        shift = at2 + 32 * k + HALF * d + w * core
                        moved = turn(rows[which][2 * f + k], shift)
                        edges[d][f] = jnp.where(mask, moved, edges[d][f])
    for i, (f, k) in enumerate(FK):
        side[f, k] = sides[i]
    for f in range(NF):
        first_up[f] = edges[0][f]
        first_down[f] = edges[1][f]

    def out(head, rest):
        return lambda j: (head, NF) if j == 0 else (rest, 2 * NF * (j - 1))

    pack_rows(t0, (out(first_up, rest_up), out(first_down, rest_down)), WS, lane, core)


def side_kernel(side, low, high, t1, y, up1, down1):
    lane, core = lanes()
    for k in range(2):
        place = (lane - 32 * k) & (LANES - 1)
        for f in range(NF):
            with_high = jnp.where(
                (place >= HALF) & (place < HALF + CORNER), high[f], side[f, k]
            )
            y[f, k] = jnp.where(place < CORNER, low[f], with_high)
    pack_rows(
        t1, (lambda j: (up1, 2 * NF * j), lambda j: (down1, 2 * NF * j)), WC, lane, core
    )


def assemble(dst, offset, which, tile, y, edges, packed):
    lane, core = lanes()
    width = WC if which else WS
    n = width // 2
    for r in range(ROWS):
        outer = ((lane + width * (1 - core)) & (LANES - 1)) < width
        for f, k in FK:
            shift = LANES - width + width * core - tile_lane(which, r) - 32 * k
            dst[offset + width + r, f, k] = jnp.where(
                outer, turn(y[f, k], shift), tile[r, f, k]
            )
    for d in range(2):
        for away in range(width):
            w, at = corner(which)[away]
            j = width - 1 - away if d == 0 else away
            row = offset + j if d == 0 else offset + width + ROWS + j
            src, base = packed[d](j % n)
            if w:
                outer = ((lane + w * (1 - core)) & (LANES - 1)) < w
                inner = ((lane - HALF + w * core) & (LANES - 1)) < w
            for f, k in FK:
                v = src[base + 2 * f + k]
                if j >= n:
                    v = turn(v, HALF)
                if w:
                    o = turn(y[f, k], LANES - w + w * core - HALF * d - at - 32 * k)
                    i = turn(edges[d][f], HALF * d - at - 32 * k - w * core)
                    v = jnp.where(inner, i, jnp.where(outer, o, v))
                dst[row, f, k] = v


def load(ref, r):
    return [[ref[r, f, k] for f in range(NF)] for k in range(2)]


def invert(x):
    r = pltpu.reciprocal(x, approx=True)
    r = r * (2.0 - x * r)
    return r * (2.0 - x * r)


STEP = 0.025


def fluxes(v):
    rho, m1, m2, m3, en = v
    inv = STEP * invert(rho)
    v1, v2, v3 = m1 * inv, m2 * inv, m3 * inv
    a, b, c = m1 * v1, m2 * v2, m3 * v3
    p = (0.4 * STEP) * en - 0.2 * (a + b + c)
    h = en + (1.0 / STEP) * p
    m12, m13, m23 = m1 * v2, m1 * v3, m2 * v3
    return (
        (STEP * m1, a + p, m12, m13, h * v1),
        (STEP * m2, m12, b + p, m23, h * v2),
        (STEP * m3, m13, m23, c + p, h * v3),
    )


def pieces(v, want):
    prev = [[None] * 2 for _ in range(NF)]
    after = [[None] * 2 for _ in range(NF)]
    here = [[None] * 2 for _ in range(NF)]
    fl = [fluxes(v[k]) for k in range(2)]
    for f in range(NF):
        s = [(0.2 * STEP) * v[k][f] for k in range(2)]
        if "prev" in want:
            prev[f] = [s[k] - fl[k][0][f] for k in range(2)]
        if "after" in want:
            after[f] = [s[k] + fl[k][0][f] for k in range(2)]
        if "here" in want:
            ym = [s[k] - fl[k][1][f] for k in range(2)]
            yp = [s[k] + fl[k][1][f] for k in range(2)]
            zm = [s[k] - fl[k][2][f] for k in range(2)]
            zp = [s[k] + fl[k][2][f] for k in range(2)]
            zc = [
                zm[1] + pltpu.roll(zp[1], 1, 0),
                pltpu.roll(zm[0], 7, 0) + zp[0],
            ]
            here[f] = [(turn(ym[k], -1) + turn(yp[k], 1)) + zc[k] for k in range(2)]
    return prev, after, here


def flat(x):
    return tuple(x[f][k] for f, k in FK)


KEEP = 1.0 - 1.2 * STEP


def rate_pass(src, lo, hi, emit):
    _, after, _ = pieces(load(src, lo), ("after",))
    prev_after = flat(after)
    _, after, here = pieces(load(src, lo + 1), ("after", "here"))
    pend = tuple(a + b for a, b in zip(flat(here), prev_after))

    def body(r, carry):
        pend, prev_after = carry
        prev, after, here = pieces(load(src, r), ("prev", "after", "here"))
        emit(r - 1, [a + b for a, b in zip(pend, flat(prev))])
        return tuple(a + b for a, b in zip(flat(here), prev_after)), flat(after)

    pend, _ = lax.fori_loop(lo + 2, hi - 1, body, (pend, flat(after)), unroll=UNROLL)
    prev, _, _ = pieces(load(src, hi - 1), ("prev",))
    emit(hi - 2, [a + b for a, b in zip(pend, flat(prev))])


def forward_kernel(
    tile, y, first_low, first_high, rest_low, rest_high, s0, u1, s1, u2, u0
):
    def packed(head, rest):
        return lambda j: (head, NF) if j == 0 else (rest, 2 * NF * (j - 1))

    assemble(
        u0, 0, 0, tile, y, (first_low, first_high),
        (packed(first_low, rest_low), packed(first_high, rest_high)),
    )

    def section(base, dst):
        def emit(r, rate):
            for (f, k), x in zip(FK, rate):
                dst[r, f, k] = KEEP * base[r, f, k] + x

        return emit

    def advance(base, sec, dst, shift):
        def emit(r, rate):
            for (f, k), x in zip(FK, rate):
                dst[r - shift, f, k] = 0.5 * (
                    base[r, f, k] + (KEEP * sec[r, f, k] + x)
                )

        return emit

    rate_pass(u0, 0, TOTAL, section(u0, s0))
    rate_pass(s0, 1, TOTAL - 1, advance(u0, s0, u1, 0))
    rate_pass(u1, 2, TOTAL - 2, section(u1, s1))
    rate_pass(s1, WS - 1, WS + ROWS + 1, advance(u1, s1, u2, WS))


def pulled(state, w, r, emit, sr=None):
    v = load(state, r if sr is None else sr)
    wm, wc, wp = load(w, r - 1), load(w, r), load(w, r + 1)
    for k in range(2):
        rho, m1, m2, m3, en = v[k]
        inv = invert(rho)
        v1, v2, v3 = m1 * inv, m2 * inv, m3 * inv
        kin = 0.5 * (v1 * v1 + v2 * v2 + v3 * v3)
        p = 0.4 * (en - rho * kin)
        h = (en + p) * inv
        d1, d2, d3, around = [], [], [], []
        for f in range(NF):
            left, right = turn(wc[k][f], 1), turn(wc[k][f], -1)
            if k == 0:
                below, above = pltpu.roll(wc[1][f], 1, 0), wc[1][f]
            else:
                below, above = wc[0][f], pltpu.roll(wc[0][f], 7, 0)
            d1.append(wp[k][f] - wm[k][f])
            d2.append(right - left)
            d3.append(above - below)
            around.append(((wp[k][f] + wm[k][f]) + (right + left)) + (above + below))
        a = [
            (m1 * d1[f] + m2 * d2[f] + m3 * d3[f]) * (1.0 if f == 0 else inv)
            for f in range(NF)
        ]
        b1, b2, b3 = [
            d[0] + v1 * d[1] + v2 * d[2] + v3 * d[3] + h * d[4] for d in (d1, d2, d3)
        ]
        pc = 0.4 * (d1[1] + d2[2] + d3[3] + a[4])
        out = [
            pc * kin - (a[1] * v1 + a[2] * v2 + a[3] * v3 + a[4] * h),
            b1 + a[1] - pc * v1,
            b2 + a[2] - pc * v2,
            b3 + a[3] - pc * v3,
            a[4] + pc,
        ]
        for f in range(NF):
            emit(f, k, out[f] + (0.2 * around[f] - 1.2 * wc[k][f]), wc[k][f])


def adjoint_kernel(
    tile0, tile1, y, first_low, first_high, low, high, s0, u1, s1, u2,
    keep_a, keep_s, send, lam, cot, wgt, lam1,
):
    assemble(
        lam, WS - WC, 1, tile1, y, (first_low, first_high),
        (lambda j: (low, 2 * NF * j), lambda j: (high, 2 * NF * j)),
    )
    lane, core = lanes()
    first = core == 0
    mine = owned(lane, core)

    def section(state, lam, lo, hi):
        def body(r, _):
            def emit(f, k, x, w):
                c = 0.0125 * x
                cot[r, f, k] = c
                wgt[r, f, k] = 0.0125 * w + 0.025 * c

            pulled(state, lam, r, emit)
            return 0

        lax.fori_loop(lo, hi, body, 0, unroll=UNROLL)

    section(s1, lam, 3, TOTAL - 3)

    def first_body(r, _):
        def emit(f, k, x, w):
            lam1[r, f, k] = lam[r, f, k] + cot[r, f, k] + x

        pulled(u1, wgt, r, emit)
        return 0

    lax.fori_loop(4, TOTAL - 4, first_body, 0, unroll=UNROLL)
    section(s0, lam1, 5, TOTAL - 5)

    def last_body(r, _):
        i = r - WS

        def emit(f, k, x, w):
            before = lam1[r, f, k]
            start = before + cot[r, f, k] + x
            mid, end = u1[r, f, k], u2[i, f, k]
            keep_a[i, f, k] = jnp.where(first, start, before)
            keep_s[i, f, k] = jnp.where(first, mid, end)
            away_a = jnp.where(first, before, start)
            away_s = jnp.where(first, end, mid)
            send[i, f, k] = jnp.where(mine, away_a, turn(away_s, HALF))

        pulled(tile0, wgt, r, emit, sr=i)
        return 0

    lax.fori_loop(WS, WS + ROWS, last_body, 0, unroll=UNROLL)


def merge_kernel(keep_a, keep_s, got, out_a, out_s):
    lane, core = lanes()
    mine = owned(lane, core)
    for f, k in FK:
        for r in range(ROWS):
            rows = pl.ds(f * 16 * ROWS + k * ROWS + r, 8, stride=2 * ROWS)
            other = got[r, f, k]
            out_a[rows, :] = jnp.where(mine, keep_a[r, f, k], other)
            out_s[rows, :] = jnp.where(mine, keep_s[r, f, k], turn(other, HALF))


def call(kernel, name, outs, scratch, *args, flops=0):
    shapes = [jax.ShapeDtypeStruct(s, jnp.float32) for s in outs]
    size = 4 * sum(a.size for a in args)
    return pl.pallas_call(
        kernel,
        out_shape=shapes,
        name=name,
        scratch_shapes=[pltpu.VMEM(s, jnp.float32) for s in scratch],
        compiler_params=pltpu.CompilerParams(vmem_limit_bytes=VMEM_LIMIT),
        cost_estimate=pl.CostEstimate(flops=flops, bytes_accessed=size, transcendentals=0),
    )(*args)


def rows_of(n):
    return (n, NF, 2, 8, LANES)


def ring(count, step):
    return [(i, (i + step) % count) for i in range(count)]


def shards(endpoints):
    shape = endpoints.shape
    tx, ty = lax.axis_size("tx"), lax.axis_size("ty")
    own = endpoints.reshape(-1, LANES)
    swap = [(0, 1), (1, 0)]
    up, down = ring(tx, 1), ring(tx, -1)
    got = lax.ppermute(own, "grp", swap)
    (mine,) = call(own_kernel, "own", [rows_of(ROWS)], [], own, flops=10**6)
    block = (NF, 2, 8, LANES)
    head, rest = (3 * NF, 8, LANES), (4 * NF, 8, LANES)
    t0, t1, first_up, first_down, rest_up, rest_down, side = call(
        pack_kernel, "pack",
        [rows_of(ROWS), rows_of(ROWS), head, head, rest, rest, block], [], mine, got,
    )
    first_low = lax.ppermute(first_up, "tx", up)
    first_high = lax.ppermute(first_down, "tx", down)
    rest_low = lax.ppermute(rest_up, "tx", up)
    rest_high = lax.ppermute(rest_down, "tx", down)
    y, up1, down1 = call(
        side_kernel, "side", [block, rest, rest], [],
        side, first_low, first_high, t1, flops=10**9,
    )
    pairs = [(i, ty + (i - 1) % ty) for i in range(ty)]
    pairs += [(b, a) for a, b in pairs]
    y = lax.ppermute(y, ("grp", "ty"), pairs)
    low1 = lax.ppermute(up1, "tx", up)
    high1 = lax.ppermute(down1, "tx", down)
    full = rows_of(TOTAL)
    s0, u1, s1, u2 = call(
        forward_kernel, "forward", [full, full, full, rows_of(ROWS)], [full],
        t0, y, first_low, first_high, rest_low, rest_high, flops=10**9,
    )
    keep_a, keep_s, send = call(
        adjoint_kernel, "adjoint", [rows_of(ROWS)] * 3, [full] * 4,
        t0, t1, y, first_low, first_high, low1, high1, s0, u1, s1, u2, flops=10**8,
    )
    other = lax.ppermute(send, "grp", swap)
    adjoints, states = call(
        merge_kernel, "merge", [own.shape, own.shape], [], keep_a, keep_s, other
    )
    return adjoints.reshape(shape), states.reshape(shape)


def solution(mesh):
    placed = P("grp", None, None, "tx", "ty")
    return jax.shard_map(
        shards, mesh=mesh, in_specs=(placed,), out_specs=(placed, placed), check_vma=False
    )
```

```python
import jax
import jax.numpy as jnp
from jax import lax
from jax.experimental import pallas as pl
from jax.experimental.pallas import tpu as pltpu
from jax.sharding import PartitionSpec as P


NF = 5
WS = 6
WC = 4
ROWS = 8
HALF = 64
LANES = 128
TOTAL = ROWS + 2 * WS
FK = [(f, k) for f in range(NF) for k in range(2)]
VMEM_LIMIT = 32 * 2**20
UNROLL = 4
UP1 = WS * NF
CORNER = WS * (WS - 1) // 2 + WC * (WC - 1) // 2


def lanes():
    lane = lax.broadcasted_iota(jnp.int32, (8, LANES), 1)
    core = lax.axis_index("grp")
    return lane, core


def owned(lane, core):
    return ((lane + HALF * core) & (LANES - 1)) < HALF


def turn(x, shift):
    if isinstance(shift, int):
        shift %= LANES
    else:
        shift &= LANES - 1
    return pltpu.roll(x, shift, 1)


def triangle(width, base):
    return [(w, base + w * (w - 1) // 2) for w in reversed(range(width))]


def corner(which):
    return triangle(WS, 0) if which == 0 else triangle(WC, WS * (WS - 1) // 2)


def tile_lane(which, r):
    if which == 0:
        return CORNER + WS * r if r < 5 else HALF + CORNER + WS * (r - 5)
    if r < 3:
        return CORNER + 5 * WS + WC * r
    return HALF + CORNER + 3 * WS + WC * (r - 3)


def own_kernel(own, rows_out):
    for f, k in FK:
        for r in range(ROWS):
            rows = pl.ds(f * 16 * ROWS + k * ROWS + r, 8, stride=2 * ROWS)
            rows_out[r, f, k] = own[rows, :]


def pack_rows(tile, out, start, n, pairs, base, lane, core):
    mine = owned(lane, core)
    for i, j in enumerate(pairs):
        for f, k in FK:
            other = turn(tile[start + n + j, f, k], HALF)
            at = base + 2 * NF * i + 2 * f + k
            out[at] = jnp.where(mine, tile[start + j, f, k], other)


def first_kernel(own, got, t0, t1, first_up, first_down):
    lane, core = lanes()
    first = core == 0
    zero = jnp.zeros((8, LANES), jnp.float32)
    edges = [[zero] * NF for _ in range(2)]
    for r in range(ROWS):
        rows = [[], []]
        for f, k in FK:
            at = pl.ds(f * 16 * ROWS + k * ROWS + r, 8, stride=2 * ROWS)
            a, b = own[r, f, k], got[at, :]
            rows[0].append(jnp.where(first, a, b))
            rows[1].append(jnp.where(first, b, a))
            t0[r, f, k] = rows[0][-1]
            t1[r, f, k] = rows[1][-1]
        for which, width in ((0, WS), (1, WC)):
            for d, away in ((0, ROWS - 1 - r), (1, r)):
                if away >= width:
                    continue
                w, at = corner(which)[away]
                if w == 0:
                    continue
                for k in range(2):
                    place = (lane - 32 * k) & (HALF - 1)
                    mask = (place >= at) & (place < at + w)
                    for f in range(NF):
                        shift = at + 32 * k + HALF * d + w * core
                        moved = turn(rows[which][2 * f + k], shift)
                        edges[d][f] = jnp.where(mask, moved, edges[d][f])
    for f in range(NF):
        first_up[f] = edges[0][f]
        first_down[f] = edges[1][f]


def rest_kernel(t0, t1, side, rest_up, rest_down):
    lane, core = lanes()
    pack_rows(t0, rest_up, ROWS - WS, WS // 2, (0, 1, 2), 0, lane, core)
    pack_rows(t0, rest_down, 0, WS // 2, (0, 1, 2), 0, lane, core)
    sides = [jnp.zeros((8, LANES), jnp.float32) for _ in FK]
    for r in range(ROWS):
        for which, width, tile in ((0, WS, t0), (1, WC, t1)):
            at = tile_lane(which, r)
            for k in range(2):
                place = (lane - 32 * k) & (LANES - 1)
                mask = (place >= at) & (place < at + width)
                for f in range(NF):
                    i = 2 * f + k
                    moved = turn(tile[r, f, k], at + 32 * k + width * core)
                    sides[i] = jnp.where(mask, moved, sides[i])
    for i, (f, k) in enumerate(FK):
        side[f, k] = sides[i]


def side_kernel(side, low, high, t1, y, up1, down1):
    lane, core = lanes()
    for k in range(2):
        place = (lane - 32 * k) & (LANES - 1)
        for f in range(NF):
            with_high = jnp.where(
                (place >= HALF) & (place < HALF + CORNER), high[f], side[f, k]
            )
            y[f, k] = jnp.where(place < CORNER, low[f], with_high)
    pack_rows(t1, up1, ROWS - WC, WC // 2, (0, 1), 0, lane, core)
    pack_rows(t1, down1, 0, WC // 2, (0, 1), 0, lane, core)


def assemble_tile(dst, offset, which, tile, y):
    lane, core = lanes()
    width = WC if which else WS
    for r in range(ROWS):
        outer = ((lane + width * (1 - core)) & (LANES - 1)) < width
        for f, k in FK:
            shift = LANES - width + width * core - tile_lane(which, r) - 32 * k
            dst[offset + r, f, k] = jnp.where(outer, turn(y[f, k], shift), tile[r, f, k])


def assemble_halo(dst, offset, which, d, y, edges, packed):
    lane, core = lanes()
    mine = owned(lane, core)
    width = WC if which else WS
    n = width // 2
    for away in range(width):
        w, at = corner(which)[away]
        j = away if d else width - 1 - away
        src, base = packed(j % n)
        if w:
            outer = ((lane + w * (1 - core)) & (LANES - 1)) < w
            inner = ((lane - HALF + w * core) & (LANES - 1)) < w
        for f, k in FK:
            v = src[base + 2 * f + k]
            if j >= n:
                v = turn(v, HALF)
            if w:
                o = turn(y[f, k], LANES - w + w * core - HALF * d - at - 32 * k)
                i = turn(edges[f], HALF * d - at - 32 * k - w * core)
                v = jnp.where(inner, i, jnp.where(outer, o, v))
            dst[offset + j, f, k] = v


def halo_kernel(t0, t1, y, first_low, first_high, rest_low, rest_high, u0, lam):
    assemble_halo(u0, 0, 0, 0, y, first_low, lambda j: (rest_low, 2 * NF * j))
    assemble_tile(u0, WS, 0, t0, y)
    assemble_halo(u0, WS + ROWS, 0, 1, y, first_high, lambda j: (rest_high, 2 * NF * j))
    assemble_tile(lam, WS, 1, t1, y)


def load(ref, r):
    return [[ref[r, f, k] for f in range(NF)] for k in range(2)]


def invert(x):
    return pltpu.reciprocal(x, approx=True)


STEP = 0.025


def fluxes(v):
    rho, m1, m2, m3, en = v
    inv = STEP * invert(rho)
    v1, v2, v3 = m1 * inv, m2 * inv, m3 * inv
    a, b, c = m1 * v1, m2 * v2, m3 * v3
    p = (0.4 * STEP) * en - 0.2 * (a + b + c)
    h = en + (1.0 / STEP) * p
    m12, m13, m23 = m1 * v2, m1 * v3, m2 * v3
    return (
        (STEP * m1, a + p, m12, m13, h * v1),
        (STEP * m2, m12, b + p, m23, h * v2),
        (STEP * m3, m13, m23, c + p, h * v3),
    )


def pieces(v, along_y=True):
    before, after, here, left, right = [], [], [], [], []
    fl = [fluxes(v[k]) for k in range(2)]
    for f in range(NF):
        s = [(0.2 * STEP) * v[k][f] for k in range(2)]
        before += [s[k] - fl[k][0][f] for k in range(2)]
        after += [s[k] + fl[k][0][f] for k in range(2)]
        if along_y:
            zm = [s[k] - fl[k][2][f] for k in range(2)]
            zp = [s[k] + fl[k][2][f] for k in range(2)]
            here += [
                zm[1] + pltpu.roll(zp[1], 1, 0),
                pltpu.roll(zm[0], 7, 0) + zp[0],
            ]
            left += [s[k] - fl[k][1][f] for k in range(2)]
            right += [s[k] + fl[k][1][f] for k in range(2)]
    return before, after, here, left, right


KEEP = 1.0 - 1.2 * STEP


def rate_pass(src, lo, hi, emit):
    _, edge, _, _, _ = pieces(load(src, lo), False)
    _, after, here, left, right = pieces(load(src, lo + 1))
    here = [a + b for a, b in zip(here, edge)]

    def done(here, left, right, before):
        return [
            (turn(a, -1) + turn(b, 1)) + (c + d)
            for a, b, c, d in zip(left, right, here, before)
        ]

    def body(r, carry):
        here, after, left, right = carry
        before, after2, here2, left2, right2 = pieces(load(src, r))
        emit(r - 1, done(here, left, right, before))
        here2 = [a + b for a, b in zip(here2, after)]
        return here2, after2, left2, right2

    here, _, left, right = lax.fori_loop(
        lo + 2, hi - 1, body, (here, after, left, right), unroll=UNROLL
    )
    before, _, _, _, _ = pieces(load(src, hi - 1), False)
    emit(hi - 2, done(here, left, right, before))


def forward_kernel(u0, s0, u1, s1, u2):
    def section(base, dst):
        def emit(r, rate):
            for (f, k), x in zip(FK, rate):
                dst[r, f, k] = KEEP * base[r, f, k] + x

        return emit

    def advance(base, sec, dst, shift):
        def emit(r, rate):
            for (f, k), x in zip(FK, rate):
                dst[r - shift, f, k] = 0.5 * (
                    base[r, f, k] + (KEEP * sec[r, f, k] + x)
                )

        return emit

    rate_pass(u0, 0, TOTAL, section(u0, s0))
    rate_pass(s0, 1, TOTAL - 1, advance(u0, s0, u1, 0))
    rate_pass(u1, 2, TOTAL - 2, section(u1, s1))
    rate_pass(s1, WS - 1, WS + ROWS + 1, advance(u1, s1, u2, WS))


def beside_lanes(row):
    diff, total = [[], []], [[], []]
    for k in range(2):
        for x in row[k]:
            before, after = turn(x, 1), turn(x, -1)
            diff[k].append(after - before)
            total[k].append(after + before)
    return diff, total


def pulled(v, wm, wc, wp, diff, total, emit):
    for k in range(2):
        rho, m1, m2, m3, en = v[k]
        inv = invert(rho)
        v1, v2, v3 = m1 * inv, m2 * inv, m3 * inv
        kin = 0.5 * (v1 * v1 + v2 * v2 + v3 * v3)
        h = 1.4 * (en * inv) - 0.4 * kin
        d1, d2, d3, around = [], diff[k], [], []
        for f in range(NF):
            if k == 0:
                below, above = pltpu.roll(wc[1][f], 1, 0), wc[1][f]
            else:
                below, above = wc[0][f], pltpu.roll(wc[0][f], 7, 0)
            d1.append(wp[k][f] - wm[k][f])
            d3.append(above - below)
            around.append(((wp[k][f] + wm[k][f]) + total[k][f]) + (above + below))
        a = [v1 * d1[f] + v2 * d2[f] + v3 * d3[f] for f in range(1, NF)]
        b1, b2, b3 = [
            d[0] + v1 * d[1] + v2 * d[2] + v3 * d[3] + h * d[4] for d in (d1, d2, d3)
        ]
        pc = 0.4 * (d1[1] + d2[2] + d3[3] + a[3])
        out = [
            pc * kin - (a[0] * v1 + a[1] * v2 + a[2] * v3 + a[3] * h),
            b1 + a[0] - pc * v1,
            b2 + a[1] - pc * v2,
            b3 + a[2] - pc * v3,
            a[3] + pc,
        ]
        for f in range(NF):
            emit(f, k, out[f] + (0.2 * around[f] - 1.2 * wc[k][f]), wc[k][f])


def pull_pass(state, w, lo, hi, emit, shift=0):
    def body(r, carry):
        wp = load(w, r + 1)
        ahead = beside_lanes(wp)
        pulled(
            load(state, r - shift), load(w, r - 1), load(w, r), wp, *carry,
            lambda f, k, x, c: emit(r, f, k, x, c),
        )
        return ahead

    lax.fori_loop(lo, hi, body, beside_lanes(load(w, lo)), unroll=UNROLL)


def adjoint_kernel(
    low_lam, tile0, y, first_low, first_high, low, high, s0, u1, s1, u2,
    keep_a, keep_s, send, lam, cot, wgt, lam1,
):
    assemble_halo(lam, WS - WC, 1, 0, y, first_low, lambda j: (low, 2 * NF * j))
    assemble_halo(lam, WS + ROWS, 1, 1, y, first_high, lambda j: (high, 2 * NF * j))
    lane, core = lanes()
    first = core == 0
    mine = owned(lane, core)

    def section(r, f, k, x, w):
        c = 0.0125 * x
        cot[r, f, k] = c
        wgt[r, f, k] = 0.0125 * w + 0.025 * c

    def middle(r, f, k, x, w):
        lam1[r, f, k] = lam[r, f, k] + (cot[r, f, k] + x)

    def last(r, f, k, x, w):
        i = r - WS
        before = lam1[r, f, k]
        start = before + (cot[r, f, k] + x)
        mid, end = u1[r, f, k], u2[i, f, k]
        keep_a[i, f, k] = jnp.where(first, start, before)
        keep_s[i, f, k] = jnp.where(first, mid, end)
        away_a = jnp.where(first, before, start)
        away_s = jnp.where(first, end, mid)
        send[i, f, k] = jnp.where(mine, away_a, turn(away_s, HALF))

    pull_pass(s1, lam, 3, TOTAL - 3, section)
    pull_pass(u1, wgt, 4, TOTAL - 4, middle)
    pull_pass(s0, lam1, 5, TOTAL - 5, section)
    pull_pass(tile0, wgt, WS, WS + ROWS, last, shift=WS)


def merge_kernel(keep_a, keep_s, got, out_a, out_s):
    lane, core = lanes()
    mine = owned(lane, core)
    for f, k in FK:
        for r in range(ROWS):
            rows = pl.ds(f * 16 * ROWS + k * ROWS + r, 8, stride=2 * ROWS)
            other = got[r, f, k]
            out_a[rows, :] = jnp.where(mine, keep_a[r, f, k], other)
            out_s[rows, :] = jnp.where(mine, keep_s[r, f, k], turn(other, HALF))


def call(kernel, name, outs, scratch, *args, flops=0, aliases=None):
    shapes = [jax.ShapeDtypeStruct(s, jnp.float32) for s in outs]
    size = 4 * sum(a.size for a in args)
    return pl.pallas_call(
        kernel,
        out_shape=shapes,
        name=name,
        scratch_shapes=[pltpu.VMEM(s, jnp.float32) for s in scratch],
        input_output_aliases=aliases or {},
        compiler_params=pltpu.CompilerParams(vmem_limit_bytes=VMEM_LIMIT),
        cost_estimate=pl.CostEstimate(flops=flops, bytes_accessed=size, transcendentals=0),
    )(*args)


def rows_of(n):
    return (n, NF, 2, 8, LANES)


def ring(count, step):
    return [(i, (i + step) % count) for i in range(count)]


def shards(endpoints):
    shape = endpoints.shape
    tx, ty = lax.axis_size("tx"), lax.axis_size("ty")
    own = endpoints.reshape(-1, LANES)
    swap = [(0, 1), (1, 0)]
    up, down = ring(tx, 1), ring(tx, -1)
    tile, full = rows_of(ROWS), rows_of(TOTAL)
    block = (NF, 2, 8, LANES)

    def pack(rows):
        return (NF * rows, 8, LANES)

    edge = (NF, 8, LANES)
    got = lax.ppermute(own, "grp", swap)
    (mine,) = call(own_kernel, "own", [tile], [], own, flops=10**6)
    t0, t1, first_up, first_down = call(
        first_kernel, "first", [tile, tile, edge, edge], [], mine, got,
        flops=10**6,
    )
    first_low = lax.ppermute(first_up, "tx", up)
    first_high = lax.ppermute(first_down, "tx", down)
    side, rest_up, rest_down = call(
        rest_kernel, "rest", [block, pack(WS), pack(WS)], [], t0, t1, flops=10**6
    )
    rest_low = lax.ppermute(rest_up, "tx", up)
    rest_high = lax.ppermute(rest_down, "tx", down)
    y, up1, down1 = call(
        side_kernel, "side", [block, pack(WC), pack(WC)], [],
        side, first_low, first_high, t1, flops=10**10,
    )
    pairs = [(i, ty + (i - 1) % ty) for i in range(ty)]
    pairs += [(b, a) for a, b in pairs]
    y = lax.ppermute(y, ("grp", "ty"), pairs)
    low1 = lax.ppermute(up1, "tx", up)
    high1 = lax.ppermute(down1, "tx", down)
    u0, lam = call(
        halo_kernel, "halo", [full, full], [],
        t0, t1, y, first_low, first_high, rest_low, rest_high, flops=10**7,
    )
    s0, u1, s1, u2 = call(
        forward_kernel, "forward", [full, full, full, tile], [], u0, flops=10**9,
    )
    keep_a, keep_s, send, _ = call(
        adjoint_kernel, "adjoint", [tile, tile, tile, full], [full] * 3,
        lam, t0, y, first_low, first_high, low1, high1, s0, u1, s1, u2, flops=10**8, aliases={0: 3},
    )
    other = lax.ppermute(send, "grp", swap)
    adjoints, states = call(
        merge_kernel, "merge", [own.shape, own.shape], [], keep_a, keep_s, other
    )
    return adjoints.reshape(shape), states.reshape(shape)


def solution(mesh):
    placed = P("grp", None, None, "tx", "ty")
    return jax.shard_map(
        shards, mesh=mesh, in_specs=(placed,), out_specs=(placed, placed), check_vma=False
    )
```

```python
import jax
import jax.numpy as jnp
from jax import lax
from jax.experimental import pallas as pl
from jax.experimental.pallas import tpu as pltpu
from jax.sharding import PartitionSpec as P


NF = 5
WS = 6
WC = 4
ROWS = 8
HALF = 64
LANES = 128
TOTAL = ROWS + 2 * WS
FK = [(f, k) for f in range(NF) for k in range(2)]
VMEM_LIMIT = 32 * 2**20
TURNS = (18, 16, 14, 8)
BACK = (14, 12, 10, 8)
UP1 = WS * NF
CORNER = WS * (WS - 1) // 2 + WC * (WC - 1) // 2


def lanes():
    lane = lax.broadcasted_iota(jnp.int32, (8, LANES), 1)
    core = lax.axis_index("grp")
    return lane, core


def owned(lane, core):
    return ((lane + HALF * core) & (LANES - 1)) < HALF


def turn(x, shift):
    if isinstance(shift, int):
        shift %= LANES
    else:
        shift &= LANES - 1
    return pltpu.roll(x, shift, 1)


def triangle(width, base):
    return [(w, base + w * (w - 1) // 2) for w in reversed(range(width))]


def corner(which):
    return triangle(WS, 0) if which == 0 else triangle(WC, WS * (WS - 1) // 2)


def tile_lane(which, r):
    if which == 0:
        return CORNER + WS * r if r < 5 else HALF + CORNER + WS * (r - 5)
    if r < 3:
        return CORNER + 5 * WS + WC * r
    return HALF + CORNER + 3 * WS + WC * (r - 3)


def own_kernel(own, rows_out):
    for f, k in FK:
        for r in range(ROWS):
            rows = pl.ds(f * 16 * ROWS + k * ROWS + r, 8, stride=2 * ROWS)
            rows_out[r, f, k] = own[rows, :]


def pack_rows(tile, out, start, n, pairs, base, lane, core):
    mine = owned(lane, core)
    for i, j in enumerate(pairs):
        for f, k in FK:
            other = turn(tile[start + n + j, f, k], HALF)
            at = base + 2 * NF * i + 2 * f + k
            out[at] = jnp.where(mine, tile[start + j, f, k], other)


def first_kernel(own, got, t0, t1, first_up, first_down):
    lane, core = lanes()
    first = core == 0
    zero = jnp.zeros((8, LANES), jnp.float32)
    edges = [[zero] * NF for _ in range(2)]
    for r in range(ROWS):
        rows = [[], []]
        for f, k in FK:
            at = pl.ds(f * 16 * ROWS + k * ROWS + r, 8, stride=2 * ROWS)
            a, b = own[r, f, k], got[at, :]
            rows[0].append(jnp.where(first, a, b))
            rows[1].append(jnp.where(first, b, a))
            t0[r, f, k] = rows[0][-1]
            t1[r, f, k] = rows[1][-1]
        for which, width in ((0, WS), (1, WC)):
            for d, away in ((0, ROWS - 1 - r), (1, r)):
                if away >= width:
                    continue
                w, at = corner(which)[away]
                if w == 0:
                    continue
                for k in range(2):
                    place = (lane - 32 * k) & (HALF - 1)
                    mask = (place >= at) & (place < at + w)
                    for f in range(NF):
                        shift = at + 32 * k + HALF * d + w * core
                        moved = turn(rows[which][2 * f + k], shift)
                        edges[d][f] = jnp.where(mask, moved, edges[d][f])
    for f in range(NF):
        first_up[f] = edges[0][f]
        first_down[f] = edges[1][f]
    pack_rows(t1, first_up, ROWS - WC, WC // 2, (0,), NF, lane, core)
    pack_rows(t1, first_down, 0, WC // 2, (0,), NF, lane, core)


def rest_kernel(t0, t1, side, rest_up, rest_down):
    lane, core = lanes()
    pack_rows(t0, rest_up, ROWS - WS, WS // 2, (0, 1, 2), 0, lane, core)
    pack_rows(t0, rest_down, 0, WS // 2, (0, 1, 2), 0, lane, core)
    sides = [jnp.zeros((8, LANES), jnp.float32) for _ in FK]
    for r in range(ROWS):
        for which, width, tile in ((0, WS, t0), (1, WC, t1)):
            at = tile_lane(which, r)
            for k in range(2):
                place = (lane - 32 * k) & (LANES - 1)
                mask = (place >= at) & (place < at + width)
                for f in range(NF):
                    i = 2 * f + k
                    moved = turn(tile[r, f, k], at + 32 * k + width * core)
                    sides[i] = jnp.where(mask, moved, sides[i])
    for i, (f, k) in enumerate(FK):
        side[f, k] = sides[i]


def side_kernel(side, low, high, t1, y, up1, down1):
    lane, core = lanes()
    for k in range(2):
        place = (lane - 32 * k) & (LANES - 1)
        for f in range(NF):
            with_high = jnp.where(
                (place >= HALF) & (place < HALF + CORNER), high[f], side[f, k]
            )
            y[f, k] = jnp.where(place < CORNER, low[f], with_high)
    pack_rows(t1, up1, ROWS - WC, WC // 2, (1,), 0, lane, core)
    pack_rows(t1, down1, 0, WC // 2, (1,), 0, lane, core)


def units(which):
    return [0.5 / u for u in UNIT] if which else UNIT


def assemble_tile(dst, offset, which, tile, y):
    lane, core = lanes()
    width = WC if which else WS
    unit = units(which)
    for r in range(ROWS):
        outer = ((lane + width * (1 - core)) & (LANES - 1)) < width
        for f, k in FK:
            shift = LANES - width + width * core - tile_lane(which, r) - 32 * k
            v = jnp.where(outer, turn(y[f, k], shift), tile[r, f, k])
            dst[offset + r, f, k] = v * unit[f]


def assemble_halo(dst, offset, which, d, y, edges, packed):
    lane, core = lanes()
    mine = owned(lane, core)
    width = WC if which else WS
    unit = units(which)
    n = width // 2
    for away in range(width):
        w, at = corner(which)[away]
        j = away if d else width - 1 - away
        src, base = packed(j % n)
        if w:
            outer = ((lane + w * (1 - core)) & (LANES - 1)) < w
            inner = ((lane - HALF + w * core) & (LANES - 1)) < w
        for f, k in FK:
            v = src[base + 2 * f + k]
            if j >= n:
                v = turn(v, HALF)
            if w:
                o = turn(y[f, k], LANES - w + w * core - HALF * d - at - 32 * k)
                i = turn(edges[f], HALF * d - at - 32 * k - w * core)
                v = jnp.where(inner, i, jnp.where(outer, o, v))
            dst[offset + j, f, k] = v * unit[f]


def halo_kernel(t0, t1, y, first_low, first_high, rest_low, rest_high, u0, lam):
    assemble_halo(u0, 0, 0, 0, y, first_low, lambda j: (rest_low, 2 * NF * j))
    assemble_tile(u0, WS, 0, t0, y)
    assemble_halo(u0, WS + ROWS, 0, 1, y, first_high, lambda j: (rest_high, 2 * NF * j))
    assemble_tile(lam, WS, 1, t1, y)


def load(ref, r):
    return [[ref[r, f, k] for f in range(NF)] for k in range(2)]


def invert(x):
    return pltpu.reciprocal(x, approx=True)


STEP = 0.025
UNIT = (1.0, STEP, STEP, STEP, STEP * STEP)
VISC = 0.2 * STEP
KEEP = 1.0 - 6.0 * VISC


def fluxes(v):
    rho, m1, m2, m3, en = v
    inv = invert(rho)
    v1, v2, v3 = m1 * inv, m2 * inv, m3 * inv
    a, b, c = m1 * v1, m2 * v2, m3 * v3
    p = 0.4 * en - 0.2 * (a + b + c)
    h = en + p
    m12, m13, m23 = m1 * v2, m1 * v3, m2 * v3
    return (
        (m1, a + p, m12, m13, h * v1),
        (m2, m12, b + p, m23, h * v2),
        (m3, m13, m23, c + p, h * v3),
    )


def pieces(v, along_y=True):
    before, after, here, left, right = [], [], [], [], []
    fl = [fluxes(v[k]) for k in range(2)]
    for f in range(NF):
        s = [VISC * v[k][f] for k in range(2)]
        before += [s[k] - fl[k][0][f] for k in range(2)]
        after += [s[k] + fl[k][0][f] for k in range(2)]
        if along_y:
            zm = [s[k] - fl[k][2][f] for k in range(2)]
            zp = [s[k] + fl[k][2][f] for k in range(2)]
            here += [
                zm[1] + pltpu.roll(zp[1], 1, 0),
                pltpu.roll(zm[0], 7, 0) + zp[0],
            ]
            left += [s[k] - fl[k][1][f] for k in range(2)]
            right += [s[k] + fl[k][1][f] for k in range(2)]
    return before, after, here, left, right


def rate_pass(src, lo, hi, emit, unroll):
    _, after, _, _, _ = pieces(load(src, lo), False)
    zero = [jnp.zeros((8, LANES), jnp.float32) for _ in FK]

    def done(here, left, right, before):
        return [
            (turn(a, -1) + turn(b, 1)) + (c + d)
            for a, b, c, d in zip(left, right, here, before)
        ]

    def body(r, carry):
        here, after, left, right = carry
        before, after2, here2, left2, right2 = pieces(load(src, r))
        emit(r - 1, done(here, left, right, before))
        here2 = [a + b for a, b in zip(here2, after)]
        return here2, after2, left2, right2

    here, _, left, right = lax.fori_loop(
        lo + 1, hi - 1, body, (zero, after, zero, zero), unroll=unroll
    )
    before, _, _, _, _ = pieces(load(src, hi - 1), False)
    emit(hi - 2, done(here, left, right, before))


def forward_kernel(u0, s0, u1, s1, u2):
    def section(base, dst):
        def emit(r, rate):
            for (f, k), x in zip(FK, rate):
                dst[r, f, k] = KEEP * base[r, f, k] + x

        return emit

    def advance(base, sec, dst, shift):
        def emit(r, rate):
            for (f, k), x in zip(FK, rate):
                dst[r - shift, f, k] = 0.5 * (
                    base[r, f, k] + (KEEP * sec[r, f, k] + x)
                )

        return emit

    rate_pass(u0, 0, TOTAL, section(u0, s0), TURNS[0])
    rate_pass(s0, 1, TOTAL - 1, advance(u0, s0, u1, 0), TURNS[1])
    rate_pass(u1, 2, TOTAL - 2, section(u1, s1), TURNS[2])
    rate_pass(s1, WS - 1, WS + ROWS + 1, advance(u1, s1, u2, WS - 1), TURNS[3])


def beside_lanes(row):
    diff, total = [[], []], [[], []]
    for k in range(2):
        for x in row[k]:
            before, after = turn(x, 1), turn(x, -1)
            diff[k].append(after - before)
            total[k].append(after + before)
    return diff, total


def pulled(v, wm, wc, wp, diff, total, emit):
    for k in range(2):
        rho, m1, m2, m3, en = v[k]
        inv = invert(rho)
        v1, v2, v3 = m1 * inv, m2 * inv, m3 * inv
        kin = 0.5 * (v1 * v1 + v2 * v2 + v3 * v3)
        h = 1.4 * (en * inv) - 0.4 * kin
        d1, d2, d3, around = [], diff[k], [], []
        for f in range(NF):
            if k == 0:
                below, above = pltpu.roll(wc[1][f], 1, 0), wc[1][f]
            else:
                below, above = wc[0][f], pltpu.roll(wc[0][f], 7, 0)
            d1.append(wp[k][f] - wm[k][f])
            d3.append(above - below)
            around.append(((wp[k][f] + wm[k][f]) + total[k][f]) + (above + below))
        a = [v1 * d1[f] + v2 * d2[f] + v3 * d3[f] for f in range(1, NF)]
        b1, b2, b3 = [
            d[0] + v1 * d[1] + v2 * d[2] + v3 * d[3] + h * d[4] for d in (d1, d2, d3)
        ]
        pc = 0.4 * (d1[1] + d2[2] + d3[3] + a[3])
        out = [
            pc * kin - (a[0] * v1 + a[1] * v2 + a[2] * v3 + a[3] * h),
            b1 + a[0] - pc * v1,
            b2 + a[1] - pc * v2,
            b3 + a[2] - pc * v3,
            a[3] + pc,
        ]
        for f in range(NF):
            emit(f, k, out[f] + (VISC * around[f] - (6.0 * VISC) * wc[k][f]), wc[k][f])


def pull_pass(state, w, lo, hi, emit, unroll):
    def body(r, carry):
        wp = load(w, r + 1)
        ahead = beside_lanes(wp)
        pulled(
            load(state, r), load(w, r - 1), load(w, r), wp, *carry,
            lambda f, k, x, c: emit(r, f, k, x, c),
        )
        return ahead

    lax.fori_loop(lo, hi, body, beside_lanes(load(w, lo)), unroll=unroll)


def adjoint_kernel(
    low_lam, u0, y, first_low, first_high, low, high, s0, u1, s1, u2,
    keep_a, keep_s, send, lam, cot, wgt, lam1,
):
    assemble_halo(lam, WS - WC, 1, 0, y, first_low, lambda j: (low, 0) if j else (first_low, NF))
    assemble_halo(lam, WS + ROWS, 1, 1, y, first_high, lambda j: (high, 0) if j else (first_high, NF))
    lane, core = lanes()
    first = core == 0
    mine = owned(lane, core)

    def section(r, f, k, x, w):
        cot[r, f, k] = x
        wgt[r, f, k] = w + x

    def middle(r, f, k, x, w):
        lam1[r, f, k] = lam[r, f, k] + 0.5 * (cot[r, f, k] + x)

    def last(r, f, k, x, w):
        i = r - WS
        before = lam1[r, f, k]
        start = before + 0.5 * (cot[r, f, k] + x)
        mid, end = u1[r, f, k], u2[i + 1, f, k]
        keep_a[i, f, k] = jnp.where(first, start, before)
        keep_s[i, f, k] = jnp.where(first, mid, end)
        away_a = jnp.where(first, before, start)
        away_s = jnp.where(first, end, mid)
        send[i, f, k] = jnp.where(mine, away_a, turn(away_s, HALF))

    pull_pass(s1, lam, 3, TOTAL - 3, section, BACK[0])
    pull_pass(u1, wgt, 4, TOTAL - 4, middle, BACK[1])
    pull_pass(s0, lam1, 5, TOTAL - 5, section, BACK[2])
    pull_pass(u0, wgt, WS, WS + ROWS, last, BACK[3])


def merge_kernel(keep_a, keep_s, got, out_a, out_s):
    lane, core = lanes()
    mine = owned(lane, core)
    for f, k in FK:
        for r in range(ROWS):
            rows = pl.ds(f * 16 * ROWS + k * ROWS + r, 8, stride=2 * ROWS)
            other = got[r, f, k]
            out_a[rows, :] = jnp.where(mine, keep_a[r, f, k], other) * (2.0 * UNIT[f])
            there = jnp.where(mine, keep_s[r, f, k], turn(other, HALF))
            out_s[rows, :] = there * (1.0 / UNIT[f])


def call(kernel, name, outs, scratch, *args, flops=0, aliases=None):
    shapes = [jax.ShapeDtypeStruct(s, jnp.float32) for s in outs]
    size = 4 * sum(a.size for a in args)
    return pl.pallas_call(
        kernel,
        out_shape=shapes,
        name=name,
        scratch_shapes=[pltpu.VMEM(s, jnp.float32) for s in scratch],
        input_output_aliases=aliases or {},
        compiler_params=pltpu.CompilerParams(vmem_limit_bytes=VMEM_LIMIT),
        cost_estimate=pl.CostEstimate(flops=flops, bytes_accessed=size, transcendentals=0),
    )(*args)


def rows_of(n):
    return (n, NF, 2, 8, LANES)


def ring(count, step):
    return [(i, (i + step) % count) for i in range(count)]


def shards(endpoints):
    shape = endpoints.shape
    tx, ty = lax.axis_size("tx"), lax.axis_size("ty")
    own = endpoints.reshape(-1, LANES)
    swap = [(0, 1), (1, 0)]
    up, down = ring(tx, 1), ring(tx, -1)
    tile, full = rows_of(ROWS), rows_of(TOTAL)
    block = (NF, 2, 8, LANES)

    def pack(rows):
        return (NF * rows, 8, LANES)

    edge = (3 * NF, 8, LANES)
    got = lax.ppermute(own, "grp", swap)
    (mine,) = call(own_kernel, "own", [tile], [], own, flops=10**6)
    t0, t1, first_up, first_down = call(
        first_kernel, "first", [tile, tile, edge, edge], [], mine, got,
        flops=10**6,
    )
    first_low = lax.ppermute(first_up, "tx", up)
    first_high = lax.ppermute(first_down, "tx", down)
    side, rest_up, rest_down = call(
        rest_kernel, "rest", [block, pack(WS), pack(WS)], [], t0, t1, flops=10**6
    )
    rest_low = lax.ppermute(rest_up, "tx", up)
    rest_high = lax.ppermute(rest_down, "tx", down)
    y, up1, down1 = call(
        side_kernel, "side", [block, pack(WC - 2), pack(WC - 2)], [],
        side, first_low, first_high, t1, flops=10**10,
    )
    pairs = [(i, ty + (i - 1) % ty) for i in range(ty)]
    pairs += [(b, a) for a, b in pairs]
    y = lax.ppermute(y, ("grp", "ty"), pairs)
    low1 = lax.ppermute(up1, "tx", up)
    high1 = lax.ppermute(down1, "tx", down)
    u0, lam = call(
        halo_kernel, "halo", [full, full], [],
        t0, t1, y, first_low, first_high, rest_low, rest_high, flops=10**7,
    )
    s0, u1, s1, u2 = call(
        forward_kernel, "forward", [full, full, full, rows_of(ROWS + 1)], [], u0,
        flops=10**9,
    )
    keep_a, keep_s, send, _ = call(
        adjoint_kernel, "adjoint", [tile, tile, tile, full], [full] * 3,
        lam, u0, y, first_low, first_high, low1, high1, s0, u1, s1, u2, flops=10**8, aliases={0: 3},
    )
    other = lax.ppermute(send, "grp", swap)
    adjoints, states = call(
        merge_kernel, "merge", [own.shape, own.shape], [], keep_a, keep_s, other
    )
    return adjoints.reshape(shape), states.reshape(shape)


def solution(mesh):
    placed = P("grp", None, None, "tx", "ty")
    return jax.shard_map(
        shards, mesh=mesh, in_specs=(placed,), out_specs=(placed, placed), check_vma=False
    )
```

```python
import jax
import jax.numpy as jnp
from jax import lax
from jax.experimental import pallas as pl
from jax.experimental.pallas import tpu as pltpu
from jax.sharding import PartitionSpec as P


NF = 5
WS = 6
WC = 4
ROWS = 8
HALF = 64
LANES = 128
TOTAL = ROWS + 2 * WS
FK = [(f, k) for f in range(NF) for k in range(2)]
VMEM_LIMIT = 32 * 2**20
UP1 = WS * NF
CORNER = WS * (WS - 1) // 2 + WC * (WC - 1) // 2


def lanes():
    lane = lax.broadcasted_iota(jnp.int32, (8, LANES), 1)
    core = lax.axis_index("grp")
    return lane, core


def owned(lane, core):
    return ((lane + HALF * core) & (LANES - 1)) < HALF


def turn(x, shift):
    if isinstance(shift, int):
        shift %= LANES
    else:
        shift &= LANES - 1
    return pltpu.roll(x, shift, 1)


def triangle(width, base):
    return [(w, base + w * (w - 1) // 2) for w in reversed(range(width))]


def corner(which):
    return triangle(WS, 0) if which == 0 else triangle(WC, WS * (WS - 1) // 2)


def tile_lane(which, r):
    if which == 0:
        return CORNER + WS * r if r < 5 else HALF + CORNER + WS * (r - 5)
    if r < 3:
        return CORNER + 5 * WS + WC * r
    return HALF + CORNER + 3 * WS + WC * (r - 3)


def own_kernel(own, rows_out):
    for f, k in FK:
        for r in range(ROWS):
            rows = pl.ds(f * 16 * ROWS + k * ROWS + r, 8, stride=2 * ROWS)
            rows_out[r, f, k] = own[rows, :]


def pack_rows(tile, out, start, n, pairs, base, lane, core):
    mine = owned(lane, core)
    for i, j in enumerate(pairs):
        for f, k in FK:
            other = turn(tile[start + n + j, f, k], HALF)
            at = base + 2 * NF * i + 2 * f + k
            out[at] = jnp.where(mine, tile[start + j, f, k], other)


def first_kernel(own, got, t0, t1, first_up, first_down):
    lane, core = lanes()
    first = core == 0
    zero = jnp.zeros((8, LANES), jnp.float32)
    edges = [[zero] * NF for _ in range(2)]
    for r in range(ROWS):
        rows = [[], []]
        for f, k in FK:
            at = pl.ds(f * 16 * ROWS + k * ROWS + r, 8, stride=2 * ROWS)
            a, b = own[r, f, k], got[at, :]
            rows[0].append(jnp.where(first, a, b))
            rows[1].append(jnp.where(first, b, a))
            t0[r, f, k] = rows[0][-1]
            t1[r, f, k] = rows[1][-1]
        for which, width in ((0, WS), (1, WC)):
            for d, away in ((0, ROWS - 1 - r), (1, r)):
                if away >= width:
                    continue
                w, at = corner(which)[away]
                if w == 0:
                    continue
                for k in range(2):
                    place = (lane - 32 * k) & (HALF - 1)
                    mask = (place >= at) & (place < at + w)
                    for f in range(NF):
                        shift = at + 32 * k + HALF * d + w * core
                        moved = turn(rows[which][2 * f + k], shift)
                        edges[d][f] = jnp.where(mask, moved, edges[d][f])
    for f in range(NF):
        first_up[f] = edges[0][f]
        first_down[f] = edges[1][f]
    pack_rows(t1, first_up, ROWS - WC, WC // 2, (0, 1), NF, lane, core)


def rest_kernel(t0, rest_up, rest_down):
    lane, core = lanes()
    pack_rows(t0, rest_up, ROWS - WS, WS // 2, (0, 1, 2), 0, lane, core)
    pack_rows(t0, rest_down, 0, WS // 2, (0, 1, 2), 0, lane, core)


def tile_kernel(t0, t1, side):
    lane, core = lanes()
    sides = [jnp.zeros((8, LANES), jnp.float32) for _ in FK]
    for r in range(ROWS):
        for which, width, tile in ((0, WS, t0), (1, WC, t1)):
            at = tile_lane(which, r)
            for k in range(2):
                place = (lane - 32 * k) & (LANES - 1)
                mask = (place >= at) & (place < at + width)
                for f in range(NF):
                    i = 2 * f + k
                    moved = turn(tile[r, f, k], at + 32 * k + width * core)
                    sides[i] = jnp.where(mask, moved, sides[i])
    for i, (f, k) in enumerate(FK):
        side[f, k] = sides[i]


def side_kernel(side, low, high, t1, y, down1):
    lane, core = lanes()
    for k in range(2):
        place = (lane - 32 * k) & (LANES - 1)
        for f in range(NF):
            with_high = jnp.where(
                (place >= HALF) & (place < HALF + CORNER), high[f], side[f, k]
            )
            y[f, k] = jnp.where(place < CORNER, low[f], with_high)
    pack_rows(t1, down1, 0, WC // 2, (0, 1), 0, lane, core)


def units(which):
    return [0.5 / u for u in UNIT] if which else UNIT


def row_maker(which, tile, y, edges, packs):
    lane, core = lanes()
    width = WC if which else WS
    unit = units(which)
    n = width // 2

    def make(i):
        r = i - width
        if 0 <= r < ROWS:
            outer = ((lane + width * (1 - core)) & (LANES - 1)) < width

            def block(f, k):
                shift = LANES - width + width * core - tile_lane(which, r) - 32 * k
                return jnp.where(outer, turn(y[f, k], shift), tile[r, f, k])

        else:
            d = 0 if r < 0 else 1
            away = r - ROWS if d else -1 - r
            j = away if d else i
            w, at = corner(which)[away]
            src, base = packs[d](j % n)
            outer = ((lane + w * (1 - core)) & (LANES - 1)) < w
            inner = ((lane - HALF + w * core) & (LANES - 1)) < w

            def block(f, k):
                v = src[base + 2 * f + k]
                if j >= n:
                    v = turn(v, HALF)
                if w:
                    o = turn(y[f, k], LANES - w + w * core - HALF * d - at - 32 * k)
                    i = turn(edges[d][f], HALF * d - at - 32 * k - w * core)
                    v = jnp.where(inner, i, jnp.where(outer, o, v))
                return v

        return [[block(f, k) * unit[f] for f in range(NF)] for k in range(2)]

    return make


def load(ref, r):
    return [[ref[r, f, k] for f in range(NF)] for k in range(2)]


def invert(x):
    return pltpu.reciprocal(x, approx=True)


STEP = 0.025
UNIT = (1.0, STEP, STEP, STEP, STEP * STEP)
VISC = 0.2 * STEP
KEEP = 1.0 - 6.0 * VISC


def fluxes(v):
    rho, m1, m2, m3, en = v
    inv = invert(rho)
    v1, v2, v3 = m1 * inv, m2 * inv, m3 * inv
    a, b, c = m1 * v1, m2 * v2, m3 * v3
    p = 0.4 * en - 0.2 * (a + b + c)
    h = en + p
    m12, m13, m23 = m1 * v2, m1 * v3, m2 * v3
    return (
        (m1, a + p, m12, m13, h * v1),
        (m2, m12, b + p, m23, h * v2),
        (m3, m13, m23, c + p, h * v3),
    )


def pieces(v, along_y=True):
    before, after, here, left, right = [], [], [], [], []
    fl = [fluxes(v[k]) for k in range(2)]
    for f in range(NF):
        s = [VISC * v[k][f] for k in range(2)]
        before += [s[k] - fl[k][0][f] for k in range(2)]
        after += [s[k] + fl[k][0][f] for k in range(2)]
        if along_y:
            zm = [s[k] - fl[k][2][f] for k in range(2)]
            zp = [s[k] + fl[k][2][f] for k in range(2)]
            here += [
                zm[1] + pltpu.roll(zp[1], 1, 0),
                pltpu.roll(zm[0], 7, 0) + zp[0],
            ]
            left += [s[k] - fl[k][1][f] for k in range(2)]
            right += [s[k] + fl[k][1][f] for k in range(2)]
    return before, after, here, left, right


def rate_pass(get, lo, hi, emit):
    _, after, _, _, _ = pieces(get(lo), False)
    here = left = right = None
    for r in range(lo + 1, hi):
        before, after2, here2, left2, right2 = pieces(get(r), r < hi - 1)
        if here is not None:
            sums = zip(left, right, here, before)
            emit(r - 1, [(turn(a, -1) + turn(b, 1)) + (c + d) for a, b, c, d in sums])
        here = [a + b for a, b in zip(here2, after)]
        after, left, right = after2, left2, right2


def forward_kernel(
    t0, y, first_low, first_high, rest_low, rest_high, u0, s0, u1, s1, u2
):
    make = row_maker(
        0, t0, y, (first_low, first_high),
        (lambda j: (rest_low, 2 * NF * j), lambda j: (rest_high, 2 * NF * j)),
    )

    for r in range(TOTAL):
        v = make(r)
        for f, k in FK:
            u0[r, f, k] = v[k][f]

    def section(base, dst):
        def emit(r, rate):
            for (f, k), x in zip(FK, rate):
                dst[r, f, k] = KEEP * base[r, f, k] + x

        return emit

    def advance(base, sec, dst, shift):
        def emit(r, rate):
            for (f, k), x in zip(FK, rate):
                there = KEEP * sec[r, f, k] + x
                dst[r - shift, f, k] = 0.5 * (base[r, f, k] + there)

        return emit

    def rows(ref):
        return lambda r: load(ref, r)

    rate_pass(rows(u0), 0, TOTAL, section(u0, s0))
    rate_pass(rows(s0), 1, TOTAL - 1, advance(u0, s0, u1, 0))
    rate_pass(rows(u1), 2, TOTAL - 2, section(u1, s1))
    rate_pass(rows(s1), WS - 1, WS + ROWS + 1, advance(u1, s1, u2, WS))


def beside_lanes(row):
    diff, total = [[], []], [[], []]
    for k in range(2):
        for x in row[k]:
            before, after = turn(x, 1), turn(x, -1)
            diff[k].append(after - before)
            total[k].append(after + before)
    return diff, total


def pulled(v, wm, wc, wp, diff, total, emit):
    for k in range(2):
        rho, m1, m2, m3, en = v[k]
        inv = invert(rho)
        v1, v2, v3 = m1 * inv, m2 * inv, m3 * inv
        kin = 0.5 * (v1 * v1 + v2 * v2 + v3 * v3)
        h = 1.4 * (en * inv) - 0.4 * kin
        d1, d2, d3, around = [], diff[k], [], []
        for f in range(NF):
            if k == 0:
                below, above = pltpu.roll(wc[1][f], 1, 0), wc[1][f]
            else:
                below, above = wc[0][f], pltpu.roll(wc[0][f], 7, 0)
            d1.append(wp[k][f] - wm[k][f])
            d3.append(above - below)
            around.append(((wp[k][f] + wm[k][f]) + total[k][f]) + (above + below))
        a = [v1 * d1[f] + v2 * d2[f] + v3 * d3[f] for f in range(1, NF)]
        b1, b2, b3 = [
            d[0] + v1 * d[1] + v2 * d[2] + v3 * d[3] + h * d[4] for d in (d1, d2, d3)
        ]
        pc = 0.4 * (d1[1] + d2[2] + d3[3] + a[3])
        out = [
            pc * kin - (a[0] * v1 + a[1] * v2 + a[2] * v3 + a[3] * h),
            b1 + a[0] - pc * v1,
            b2 + a[1] - pc * v2,
            b3 + a[2] - pc * v3,
            a[3] + pc,
        ]
        for f in range(NF):
            emit(f, k, out[f] + (VISC * around[f] - (6.0 * VISC) * wc[k][f]), wc[k][f])


def pull_pass(state, w, lo, hi, emit, make=None):
    def row(r):
        if make:
            v = make(r)
            for f, k in FK:
                w[r, f, k] = v[k][f]
        return load(w, r)

    row(lo - 1)
    beside = beside_lanes(row(lo))
    for r in range(lo, hi):
        wp = row(r + 1)
        ahead = beside_lanes(wp)
        pulled(
            load(state, r), load(w, r - 1), load(w, r), wp, *beside,
            lambda f, k, x, c: emit(r, f, k, x, c),
        )
        beside = ahead


def send_block(out, i, f, k, lam, state, mine):
    out[i, f, k] = jnp.where(mine, lam, turn(state, HALF))


def last_step(s0, u0, lam1, cot, wgt, emit):
    def section(r, f, k, x, w):
        cot[r, f, k] = x
        wgt[r, f, k] = w + x

    def last(r, f, k, x, w):
        emit(r - WS, f, k, lam1[r, f, k] + 0.5 * (cot[r, f, k] + x))

    pull_pass(s0, lam1, 5, TOTAL - 5, section)
    pull_pass(u0, wgt, WS, WS + ROWS, last)


def adjoint_kernel(
    t1, y, first_low, first_high, high, u0, s0, u1, s1, u2,
    lam1, send, lam, cot, wgt,
):
    make = row_maker(
        1, t1, y, (first_low, first_high),
        (
            lambda j: (first_low, NF + 2 * NF * j),
            lambda j: (high, 2 * NF * j),
        ),
    )
    lane, core = lanes()
    mine = owned(lane, core)

    def section(r, f, k, x, w):
        cot[r, f, k] = x
        wgt[r, f, k] = w + x

    def middle(r, f, k, x, w):
        lam1[r, f, k] = lam[r, f, k] + 0.5 * (cot[r, f, k] + x)

    for r in range(2, TOTAL - 2):
        v = make(r - (WS - WC))
        for f, k in FK:
            lam[r, f, k] = v[k][f]
    pull_pass(s1, lam, 3, TOTAL - 3, section)
    pull_pass(u1, wgt, 4, TOTAL - 4, middle)

    @pl.when(core == 0)
    def _():
        for i in range(ROWS):
            for f, k in FK:
                send_block(send, i, f, k, lam1[WS + i, f, k], u2[i, f, k], mine)

    @pl.when(core == 1)
    def _():
        last_step(
            s0, u0, lam1, cot, wgt,
            lambda i, f, k, x: send_block(send, i, f, k, x, u1[WS + i, f, k], mine),
        )


def finish_kernel(lam1, u0, s0, u1, u2, keep_a, keep_s, cot, wgt):
    core = lax.axis_index("grp")

    @pl.when(core == 0)
    def _():
        def emit(i, f, k, x):
            keep_a[i, f, k] = x
            keep_s[i, f, k] = u1[WS + i, f, k]

        last_step(s0, u0, lam1, cot, wgt, emit)

    @pl.when(core == 1)
    def _():
        for i in range(ROWS):
            for f, k in FK:
                keep_a[i, f, k] = lam1[WS + i, f, k]
                keep_s[i, f, k] = u2[i, f, k]


def merge_kernel(keep_a, keep_s, got, out_a, out_s):
    lane, core = lanes()
    mine = owned(lane, core)
    for f, k in FK:
        for r in range(ROWS):
            rows = pl.ds(f * 16 * ROWS + k * ROWS + r, 8, stride=2 * ROWS)
            other = got[r, f, k]
            out_a[rows, :] = jnp.where(mine, keep_a[r, f, k], other) * (2.0 * UNIT[f])
            there = jnp.where(mine, keep_s[r, f, k], turn(other, HALF))
            out_s[rows, :] = there * (1.0 / UNIT[f])


def call(kernel, name, outs, scratch, *args, flops=0, aliases=None):
    shapes = [jax.ShapeDtypeStruct(s, jnp.float32) for s in outs]
    size = 4 * sum(a.size for a in args)
    return pl.pallas_call(
        kernel,
        out_shape=shapes,
        name=name,
        scratch_shapes=[pltpu.VMEM(s, jnp.float32) for s in scratch],
        input_output_aliases=aliases or {},
        compiler_params=pltpu.CompilerParams(vmem_limit_bytes=VMEM_LIMIT),
        cost_estimate=pl.CostEstimate(flops=flops, bytes_accessed=size, transcendentals=0),
    )(*args)


def rows_of(n):
    return (n, NF, 2, 8, LANES)


def ring(count, step):
    return [(i, (i + step) % count) for i in range(count)]


def shards(endpoints):
    shape = endpoints.shape
    tx, ty = lax.axis_size("tx"), lax.axis_size("ty")
    own = endpoints.reshape(-1, LANES)
    swap = [(0, 1), (1, 0)]
    up, down = ring(tx, 1), ring(tx, -1)
    tile, full = rows_of(ROWS), rows_of(TOTAL)
    block = (NF, 2, 8, LANES)

    def pack(rows):
        return (NF * rows, 8, LANES)

    edge = (NF, 8, LANES)
    got = lax.ppermute(own, "grp", swap)
    (mine,) = call(own_kernel, "own", [tile], [], own, flops=10**6)
    t0, t1, first_up, first_down = call(
        first_kernel, "first", [tile, tile, pack(WC + 1), edge], [], mine, got,
        flops=10**6,
    )
    first_low = lax.ppermute(first_up, "tx", up)
    first_high = lax.ppermute(first_down, "tx", down)
    rest_up, rest_down = call(
        rest_kernel, "rest", [pack(WS), pack(WS)], [], t0, flops=10**6
    )
    (side,) = call(tile_kernel, "tile", [block], [], t0, t1, flops=10**7)
    rest_low = lax.ppermute(rest_up, "tx", up)
    rest_high = lax.ppermute(rest_down, "tx", down)
    y, down1 = call(
        side_kernel, "side", [block, pack(WC)], [],
        side, first_low, first_high, t1, flops=10**10,
    )
    pairs = [(i, ty + (i - 1) % ty) for i in range(ty)]
    pairs += [(b, a) for a, b in pairs]
    y = lax.ppermute(y, ("grp", "ty"), pairs)
    high1 = lax.ppermute(down1, "tx", down)
    u0, s0, u1, s1, u2 = call(
        forward_kernel, "forward", [full, full, full, full, tile], [],
        t0, y, first_low, first_high, rest_low, rest_high, flops=10**9,
    )
    lam1, send = call(
        adjoint_kernel, "adjoint", [full, tile], [full] * 3,
        t1, y, first_low, first_high, high1, u0, s0, u1, s1, u2, flops=10**8,
    )
    other = lax.ppermute(send, "grp", swap)
    keep_a, keep_s = call(
        finish_kernel, "finish", [tile, tile], [full] * 2, lam1, u0, s0, u1, u2,
        flops=10**8,
    )
    adjoints, states = call(
        merge_kernel, "merge", [own.shape, own.shape], [], keep_a, keep_s, other
    )
    return adjoints.reshape(shape), states.reshape(shape)


def solution(mesh):
    placed = P("grp", None, None, "tx", "ty")
    return jax.shard_map(
        shards, mesh=mesh, in_specs=(placed,), out_specs=(placed, placed), check_vma=False
    )
```

```python
import jax
import jax.numpy as jnp
from jax import lax
from jax.experimental import pallas as pl
from jax.experimental.pallas import tpu as pltpu
from jax.sharding import PartitionSpec as P


NF = 5
WS = 6
WC = 4
ROWS = 8
HALF = 64
LANES = 128
TOTAL = ROWS + 2 * WS
FK = [(f, k) for f in range(NF) for k in range(2)]
VMEM_LIMIT = 32 * 2**20
UP1 = WS * NF
CORNER = WS * (WS - 1) // 2 + WC * (WC - 1) // 2


def lanes():
    lane = lax.broadcasted_iota(jnp.int32, (8, LANES), 1)
    core = lax.axis_index("grp")
    return lane, core


def owned(lane, core):
    return ((lane + HALF * core) & (LANES - 1)) < HALF


def turn(x, shift):
    if isinstance(shift, int):
        shift %= LANES
    else:
        shift &= LANES - 1
    return pltpu.roll(x, shift, 1)


def triangle(width, base):
    return [(w, base + w * (w - 1) // 2) for w in reversed(range(width))]


def corner(which):
    return triangle(WS, 0) if which == 0 else triangle(WC, WS * (WS - 1) // 2)


def tile_lane(which, r):
    if which == 0:
        return CORNER + WS * r if r < 5 else HALF + CORNER + WS * (r - 5)
    if r < 3:
        return CORNER + 5 * WS + WC * r
    return HALF + CORNER + 3 * WS + WC * (r - 3)


def own_kernel(own, rows_out):
    for f, k in FK:
        for r in range(ROWS):
            rows = pl.ds(f * 16 * ROWS + k * ROWS + r, 8, stride=2 * ROWS)
            rows_out[r, f, k] = own[rows, :]


def pack_rows(tile, out, start, n, pairs, base, lane, core):
    mine = owned(lane, core)
    for i, j in enumerate(pairs):
        for f, k in FK:
            other = turn(tile[start + n + j, f, k], HALF)
            at = base + 2 * NF * i + 2 * f + k
            out[at] = jnp.where(mine, tile[start + j, f, k], other)


def first_kernel(own, got, t0, t1, first_up, first_down):
    lane, core = lanes()
    first = core == 0
    zero = jnp.zeros((8, LANES), jnp.float32)
    edges = [[zero] * NF for _ in range(2)]
    for r in range(ROWS):
        rows = [[], []]
        for f, k in FK:
            at = pl.ds(f * 16 * ROWS + k * ROWS + r, 8, stride=2 * ROWS)
            a, b = own[r, f, k], got[at, :]
            rows[0].append(jnp.where(first, a, b))
            rows[1].append(jnp.where(first, b, a))
            t0[r, f, k] = rows[0][-1]
            t1[r, f, k] = rows[1][-1]
        for which, width in ((0, WS), (1, WC)):
            for d, away in ((0, ROWS - 1 - r), (1, r)):
                if away >= width:
                    continue
                w, at = corner(which)[away]
                if w == 0:
                    continue
                for k in range(2):
                    place = (lane - 32 * k) & (HALF - 1)
                    mask = (place >= at) & (place < at + w)
                    for f in range(NF):
                        shift = at + 32 * k + HALF * d + w * core
                        moved = turn(rows[which][2 * f + k], shift)
                        edges[d][f] = jnp.where(mask, moved, edges[d][f])
    for f in range(NF):
        first_up[f] = edges[0][f]
        first_down[f] = edges[1][f]
    pack_rows(t1, first_up, ROWS - WC, WC // 2, (0, 1), NF, lane, core)


def rest_kernel(t0, rest_up, rest_down):
    lane, core = lanes()
    pack_rows(t0, rest_up, ROWS - WS, WS // 2, (0, 1, 2), 0, lane, core)
    pack_rows(t0, rest_down, 0, WS // 2, (0, 1, 2), 0, lane, core)


def late_kernel(t1, y, down1):
    lane, core = lanes()
    pack_rows(t1, down1, 0, WC // 2, (0, 1), 0, lane, core)


def tile_kernel(t0, t1, side):
    lane, core = lanes()
    sides = [jnp.zeros((8, LANES), jnp.float32) for _ in FK]
    for r in range(ROWS):
        for which, width, tile in ((0, WS, t0), (1, WC, t1)):
            at = tile_lane(which, r)
            for k in range(2):
                place = (lane - 32 * k) & (LANES - 1)
                mask = (place >= at) & (place < at + width)
                for f in range(NF):
                    i = 2 * f + k
                    moved = turn(tile[r, f, k], at + 32 * k + width * core)
                    sides[i] = jnp.where(mask, moved, sides[i])
    for i, (f, k) in enumerate(FK):
        side[f, k] = sides[i]


def side_kernel(side, low, high, y):
    lane, core = lanes()
    for k in range(2):
        place = (lane - 32 * k) & (LANES - 1)
        for f in range(NF):
            with_high = jnp.where(
                (place >= HALF) & (place < HALF + CORNER), high[f], side[f, k]
            )
            y[f, k] = jnp.where(place < CORNER, low[f], with_high)


def units(which):
    return [0.5 / u for u in UNIT] if which else UNIT


def row_maker(which, tile, y, edges, packs):
    lane, core = lanes()
    width = WC if which else WS
    unit = units(which)
    n = width // 2

    def make(i):
        r = i - width
        if 0 <= r < ROWS:
            outer = ((lane + width * (1 - core)) & (LANES - 1)) < width

            def block(f, k):
                shift = LANES - width + width * core - tile_lane(which, r) - 32 * k
                return jnp.where(outer, turn(y[f, k], shift), tile[r, f, k])

        else:
            d = 0 if r < 0 else 1
            away = r - ROWS if d else -1 - r
            j = away if d else i
            w, at = corner(which)[away]
            src, base = packs[d](j % n)
            outer = ((lane + w * (1 - core)) & (LANES - 1)) < w
            inner = ((lane - HALF + w * core) & (LANES - 1)) < w

            def block(f, k):
                v = src[base + 2 * f + k]
                if j >= n:
                    v = turn(v, HALF)
                if w:
                    o = turn(y[f, k], LANES - w + w * core - HALF * d - at - 32 * k)
                    i = turn(edges[d][f], HALF * d - at - 32 * k - w * core)
                    v = jnp.where(inner, i, jnp.where(outer, o, v))
                return v

        return [[block(f, k) * unit[f] for f in range(NF)] for k in range(2)]

    return make


def load(ref, r):
    return [[ref[r, f, k] for f in range(NF)] for k in range(2)]


def invert(x):
    return pltpu.reciprocal(x, approx=True)


STEP = 0.025
UNIT = (1.0, STEP, STEP, STEP, STEP * STEP)
VISC = 0.2 * STEP
KEEP = 1.0 - 6.0 * VISC


def fluxes(v):
    rho, m1, m2, m3, en = v
    inv = invert(rho)
    v1, v2, v3 = m1 * inv, m2 * inv, m3 * inv
    a, b, c = m1 * v1, m2 * v2, m3 * v3
    p = 0.4 * en - 0.2 * (a + b + c)
    h = en + p
    m12, m13, m23 = m1 * v2, m1 * v3, m2 * v3
    return (
        (m1, a + p, m12, m13, h * v1),
        (m2, m12, b + p, m23, h * v2),
        (m3, m13, m23, c + p, h * v3),
    )


def pieces(v, along_y=True):
    before, after, here, left, right = [], [], [], [], []
    fl = [fluxes(v[k]) for k in range(2)]
    for f in range(NF):
        s = [VISC * v[k][f] for k in range(2)]
        before += [s[k] - fl[k][0][f] for k in range(2)]
        after += [s[k] + fl[k][0][f] for k in range(2)]
        if along_y:
            zm = [s[k] - fl[k][2][f] for k in range(2)]
            zp = [s[k] + fl[k][2][f] for k in range(2)]
            here += [
                zm[1] + pltpu.roll(zp[1], 1, 0),
                pltpu.roll(zm[0], 7, 0) + zp[0],
            ]
            left += [s[k] - fl[k][1][f] for k in range(2)]
            right += [s[k] + fl[k][1][f] for k in range(2)]
    return before, after, here, left, right


def rate_pass(get, lo, hi, emit):
    _, after, _, _, _ = pieces(get(lo), False)
    here = left = right = None
    for r in range(lo + 1, hi):
        before, after2, here2, left2, right2 = pieces(get(r), r < hi - 1)
        if here is not None:
            sums = zip(left, right, here, before)
            emit(r - 1, [(turn(a, -1) + turn(b, 1)) + (c + d) for a, b, c, d in sums])
        here = [a + b for a, b in zip(here2, after)]
        after, left, right = after2, left2, right2


def steps(u0, s0, u1, s1, u2):
    def section(base, dst):
        def emit(r, rate):
            for (f, k), x in zip(FK, rate):
                dst[r, f, k] = KEEP * base[r, f, k] + x

        return emit

    def advance(base, sec, dst, shift):
        def emit(r, rate):
            for (f, k), x in zip(FK, rate):
                there = KEEP * sec[r, f, k] + x
                dst[r - shift, f, k] = 0.5 * (base[r, f, k] + there)

        return emit

    def run(ref, emit):
        return lambda lo, hi: rate_pass(lambda r: load(ref, r), lo, hi, emit)

    return (
        run(u0, section(u0, s0)),
        run(s0, advance(u0, s0, u1, 0)),
        run(u1, section(u1, s1)),
        run(s1, advance(u1, s1, u2, WS)),
    )


def outer_forward(u0, s0, u1, s1):
    passes = steps(u0, s0, u1, s1, None)
    for n in range(3):
        passes[n](n, n + 4)
        passes[n](TOTAL - 4 - n, TOTAL - n)


def forward_kernel(
    t0, y, first_low, first_high, rest_low, rest_high, u0, s0, u1, s1, u2
):
    make = row_maker(
        0, t0, y, (first_low, first_high),
        (lambda j: (rest_low, 2 * NF * j), lambda j: (rest_high, 2 * NF * j)),
    )
    for r in range(TOTAL):
        v = make(r)
        for f, k in FK:
            u0[r, f, k] = v[k][f]
    for n, step in enumerate(steps(u0, s0, u1, s1, u2)):
        step(2 + n, TOTAL - 2 - n)

    @pl.when(lax.axis_index("grp") == 1)
    def _():
        outer_forward(u0, s0, u1, s1)


def beside_lanes(row):
    diff, total = [[], []], [[], []]
    for k in range(2):
        for x in row[k]:
            before, after = turn(x, 1), turn(x, -1)
            diff[k].append(after - before)
            total[k].append(after + before)
    return diff, total


def pulled(v, wm, wc, wp, diff, total, emit):
    for k in range(2):
        rho, m1, m2, m3, en = v[k]
        inv = invert(rho)
        v1, v2, v3 = m1 * inv, m2 * inv, m3 * inv
        kin = 0.5 * (v1 * v1 + v2 * v2 + v3 * v3)
        h = 1.4 * (en * inv) - 0.4 * kin
        d1, d2, d3, around = [], diff[k], [], []
        for f in range(NF):
            if k == 0:
                below, above = pltpu.roll(wc[1][f], 1, 0), wc[1][f]
            else:
                below, above = wc[0][f], pltpu.roll(wc[0][f], 7, 0)
            d1.append(wp[k][f] - wm[k][f])
            d3.append(above - below)
            around.append(((wp[k][f] + wm[k][f]) + total[k][f]) + (above + below))
        a = [v1 * d1[f] + v2 * d2[f] + v3 * d3[f] for f in range(1, NF)]
        b1, b2, b3 = [
            d[0] + v1 * d[1] + v2 * d[2] + v3 * d[3] + h * d[4] for d in (d1, d2, d3)
        ]
        pc = 0.4 * (d1[1] + d2[2] + d3[3] + a[3])
        out = [
            pc * kin - (a[0] * v1 + a[1] * v2 + a[2] * v3 + a[3] * h),
            b1 + a[0] - pc * v1,
            b2 + a[1] - pc * v2,
            b3 + a[2] - pc * v3,
            a[3] + pc,
        ]
        for f in range(NF):
            emit(f, k, out[f] + (VISC * around[f] - (6.0 * VISC) * wc[k][f]), wc[k][f])


def pull_pass(state, w, lo, hi, emit, make=None):
    def row(r):
        if make:
            v = make(r)
            for f, k in FK:
                w[r, f, k] = v[k][f]
        return load(w, r)

    row(lo - 1)
    beside = beside_lanes(row(lo))
    for r in range(lo, hi):
        wp = row(r + 1)
        ahead = beside_lanes(wp)
        pulled(
            load(state, r), load(w, r - 1), load(w, r), wp, *beside,
            lambda f, k, x, c: emit(r, f, k, x, c),
        )
        beside = ahead


def send_block(out, i, f, k, lam, state, mine):
    out[i, f, k] = jnp.where(mine, lam, turn(state, HALF))


def last_step(s0, u0, lam1, cot, wgt, emit):
    def section(r, f, k, x, w):
        cot[r, f, k] = x
        wgt[r, f, k] = w + x

    def last(r, f, k, x, w):
        emit(r - WS, f, k, lam1[r, f, k] + 0.5 * (cot[r, f, k] + x))

    pull_pass(s0, lam1, 5, TOTAL - 5, section)
    pull_pass(u0, wgt, WS, WS + ROWS, last)


def first_step(s1, u1, lam, cot, wgt, lam1, cuts):
    def section(r, f, k, x, w):
        cot[r, f, k] = x
        wgt[r, f, k] = w + x

    def middle(r, f, k, x, w):
        lam1[r, f, k] = lam[r, f, k] + 0.5 * (cot[r, f, k] + x)

    for lo, hi in cuts[0]:
        pull_pass(s1, lam, lo, hi, section)
    for lo, hi in cuts[1]:
        pull_pass(u1, wgt, lo, hi, middle)


INNER = (((5, TOTAL - 5),), ((6, TOTAL - 6),))
OUTER = (((3, 5), (TOTAL - 5, TOTAL - 3)), ((4, 6), (TOTAL - 6, TOTAL - 4)))


def adjoint_kernel(
    t1, y, first_low, first_high, high, u0, s0, u1, s1, u2,
    lam1, send, lam, cot, wgt,
):
    make = row_maker(
        1, t1, y, (first_low, first_high),
        (
            lambda j: (first_low, NF + 2 * NF * j),
            lambda j: (high, 2 * NF * j),
        ),
    )
    lane, core = lanes()
    mine = owned(lane, core)
    for r in range(2, TOTAL - 2):
        v = make(r - (WS - WC))
        for f, k in FK:
            lam[r, f, k] = v[k][f]
    first_step(s1, u1, lam, cot, wgt, lam1, INNER)

    @pl.when(core == 0)
    def _():
        for i in range(ROWS):
            for f, k in FK:
                send_block(send, i, f, k, lam1[WS + i, f, k], u2[i, f, k], mine)

    @pl.when(core == 1)
    def _():
        first_step(s1, u1, lam, cot, wgt, lam1, OUTER)
        last_step(
            s0, u0, lam1, cot, wgt,
            lambda i, f, k, x: send_block(send, i, f, k, x, u1[WS + i, f, k], mine),
        )


def finish_kernel(
    a, b, c, d, e, g, u0, lam, u2, keep_a, keep_s, s0, u1, s1, lam1, cot, wgt
):
    core = lax.axis_index("grp")

    @pl.when(core == 0)
    def _():
        def emit(i, f, k, x):
            keep_a[i, f, k] = x
            keep_s[i, f, k] = u1[WS + i, f, k]

        outer_forward(u0, s0, u1, s1)
        first_step(s1, u1, lam, cot, wgt, lam1, OUTER)
        last_step(s0, u0, lam1, cot, wgt, emit)

    @pl.when(core == 1)
    def _():
        for i in range(ROWS):
            for f, k in FK:
                keep_a[i, f, k] = lam1[WS + i, f, k]
                keep_s[i, f, k] = u2[i, f, k]


def merge_kernel(keep_a, keep_s, got, out_a, out_s):
    lane, core = lanes()
    mine = owned(lane, core)
    for f, k in FK:
        for r in range(ROWS):
            rows = pl.ds(f * 16 * ROWS + k * ROWS + r, 8, stride=2 * ROWS)
            other = got[r, f, k]
            out_a[rows, :] = jnp.where(mine, keep_a[r, f, k], other) * (2.0 * UNIT[f])
            there = jnp.where(mine, keep_s[r, f, k], turn(other, HALF))
            out_s[rows, :] = there * (1.0 / UNIT[f])


def call(kernel, name, outs, scratch, *args, flops=0, aliases=None):
    shapes = [jax.ShapeDtypeStruct(s, jnp.float32) for s in outs]
    size = 4 * sum(a.size for a in args)
    return pl.pallas_call(
        kernel,
        out_shape=shapes,
        name=name,
        scratch_shapes=[pltpu.VMEM(s, jnp.float32) for s in scratch],
        input_output_aliases=aliases or {},
        compiler_params=pltpu.CompilerParams(vmem_limit_bytes=VMEM_LIMIT),
        cost_estimate=pl.CostEstimate(flops=flops, bytes_accessed=size, transcendentals=0),
    )(*args)


def rows_of(n):
    return (n, NF, 2, 8, LANES)


def ring(count, step):
    return [(i, (i + step) % count) for i in range(count)]


def shards(endpoints):
    shape = endpoints.shape
    tx, ty = lax.axis_size("tx"), lax.axis_size("ty")
    own = endpoints.reshape(-1, LANES)
    swap = [(0, 1), (1, 0)]
    up, down = ring(tx, 1), ring(tx, -1)
    tile, full = rows_of(ROWS), rows_of(TOTAL)
    block = (NF, 2, 8, LANES)

    def pack(rows):
        return (NF * rows, 8, LANES)

    edge = (NF, 8, LANES)
    got = lax.ppermute(own, "grp", swap)
    (mine,) = call(own_kernel, "own", [tile], [], own, flops=10**6)
    t0, t1, first_up, first_down = call(
        first_kernel, "first", [tile, tile, pack(WC + 1), edge], [], mine, got,
        flops=10**6,
    )
    first_low = lax.ppermute(first_up, "tx", up)
    first_high = lax.ppermute(first_down, "tx", down)
    rest_up, rest_down = call(
        rest_kernel, "rest", [pack(WS), pack(WS)], [], t0, flops=10**6
    )
    (side,) = call(tile_kernel, "tile", [block], [], t0, t1, flops=10**7)
    rest_low = lax.ppermute(rest_up, "tx", up)
    rest_high = lax.ppermute(rest_down, "tx", down)
    (sent,) = call(
        side_kernel, "side", [block], [], side, first_low, first_high, flops=10**10,
    )
    (down1,) = call(late_kernel, "late", [pack(WC)], [], t1, sent, flops=10**6)
    pairs = [(i, ty + (i - 1) % ty) for i in range(ty)]
    pairs += [(b, a) for a, b in pairs]
    y = lax.ppermute(sent, ("grp", "ty"), pairs)
    high1 = lax.ppermute(down1, "tx", down)
    u0, s0, u1, s1, u2 = call(
        forward_kernel, "forward", [full, full, full, full, tile], [],
        t0, y, first_low, first_high, rest_low, rest_high, flops=10**9,
    )
    lam1, send, lam, cot, wgt = call(
        adjoint_kernel, "adjoint", [full, tile, full, full, full], [],
        t1, y, first_low, first_high, high1, u0, s0, u1, s1, u2, flops=10**8,
    )
    other = lax.ppermute(send, "grp", swap)
    keep_a, keep_s, *_ = call(
        finish_kernel, "finish", [tile, tile] + [full] * 6, [],
        s0, u1, s1, lam1, cot, wgt, u0, lam, u2,
        flops=10**8, aliases={i: i + 2 for i in range(6)},
    )
    adjoints, states = call(
        merge_kernel, "merge", [own.shape, own.shape], [], keep_a, keep_s, other
    )
    return adjoints.reshape(shape), states.reshape(shape)


def solution(mesh):
    placed = P("grp", None, None, "tx", "ty")
    return jax.shard_map(
        shards, mesh=mesh, in_specs=(placed,), out_specs=(placed, placed), check_vma=False
    )
```

```python
import jax
import jax.numpy as jnp
from jax import lax
from jax.experimental import pallas as pl
from jax.experimental.pallas import tpu as pltpu
from jax.sharding import PartitionSpec as P


NF = 5
WS = 6
WC = 4
ROWS = 8
HALF = 64
LANES = 128
TOTAL = ROWS + 2 * WS
FK = [(f, k) for f in range(NF) for k in range(2)]
VMEM_LIMIT = 32 * 2**20
UP1 = WS * NF
CORNER = WS * (WS - 1) // 2 + WC * (WC - 1) // 2


def lanes():
    lane = lax.broadcasted_iota(jnp.int32, (8, LANES), 1)
    core = lax.axis_index("grp")
    return lane, core


def owned(lane, core):
    return ((lane + HALF * core) & (LANES - 1)) < HALF


def turn(x, shift):
    if isinstance(shift, int):
        shift %= LANES
    else:
        shift &= LANES - 1
    return pltpu.roll(x, shift, 1)


def triangle(width, base):
    return [(w, base + w * (w - 1) // 2) for w in reversed(range(width))]


def corner(which):
    return triangle(WS, 0) if which == 0 else triangle(WC, WS * (WS - 1) // 2)


def tile_lane(which, r):
    if which == 0:
        return CORNER + WS * r if r < 5 else HALF + CORNER + WS * (r - 5)
    if r < 3:
        return CORNER + 5 * WS + WC * r
    return HALF + CORNER + 3 * WS + WC * (r - 3)


def own_kernel(own, rows_out):
    for f, k in FK:
        for r in range(ROWS):
            rows = pl.ds(f * 16 * ROWS + k * ROWS + r, 8, stride=2 * ROWS)
            rows_out[r, f, k] = own[rows, :]


def pack_rows(tile, out, start, n, pairs, base, lane, core):
    mine = owned(lane, core)
    for i, j in enumerate(pairs):
        for f, k in FK:
            other = turn(tile[start + n + j, f, k], HALF)
            at = base + 2 * NF * i + 2 * f + k
            out[at] = jnp.where(mine, tile[start + j, f, k], other)


def first_kernel(own, got, t0, t1, first_up, first_down):
    lane, core = lanes()
    first = core == 0
    zero = jnp.zeros((8, LANES), jnp.float32)
    edges = [[zero] * NF for _ in range(2)]
    for r in range(ROWS):
        rows = [[], []]
        for f, k in FK:
            at = pl.ds(f * 16 * ROWS + k * ROWS + r, 8, stride=2 * ROWS)
            a, b = own[r, f, k], got[at, :]
            rows[0].append(jnp.where(first, a, b))
            rows[1].append(jnp.where(first, b, a))
            t0[r, f, k] = rows[0][-1]
            t1[r, f, k] = rows[1][-1]
        for which, width in ((0, WS), (1, WC)):
            for d, away in ((0, ROWS - 1 - r), (1, r)):
                if away >= width:
                    continue
                w, at = corner(which)[away]
                if w == 0:
                    continue
                for k in range(2):
                    place = (lane - 32 * k) & (HALF - 1)
                    mask = (place >= at) & (place < at + w)
                    for f in range(NF):
                        shift = at + 32 * k + HALF * d + w * core
                        moved = turn(rows[which][2 * f + k], shift)
                        edges[d][f] = jnp.where(mask, moved, edges[d][f])
    for f in range(NF):
        first_up[f] = edges[0][f]
        first_down[f] = edges[1][f]
    pack_rows(t1, first_up, ROWS - WC, WC // 2, (0, 1), NF, lane, core)


def rest_kernel(t0, rest_up, rest_down):
    lane, core = lanes()
    pack_rows(t0, rest_up, ROWS - WS, WS // 2, (0, 1, 2), 0, lane, core)
    pack_rows(t0, rest_down, 0, WS // 2, (0, 1, 2), 0, lane, core)


def late_kernel(t1, y, down1):
    lane, core = lanes()
    pack_rows(t1, down1, 0, WC // 2, (0, 1), 0, lane, core)


def tile_kernel(t0, t1, side):
    lane, core = lanes()
    sides = [jnp.zeros((8, LANES), jnp.float32) for _ in FK]
    for r in range(ROWS):
        for which, width, tile in ((0, WS, t0), (1, WC, t1)):
            at = tile_lane(which, r)
            for k in range(2):
                place = (lane - 32 * k) & (LANES - 1)
                mask = (place >= at) & (place < at + width)
                for f in range(NF):
                    i = 2 * f + k
                    moved = turn(tile[r, f, k], at + 32 * k + width * core)
                    sides[i] = jnp.where(mask, moved, sides[i])
    for i, (f, k) in enumerate(FK):
        side[f, k] = sides[i]


def side_kernel(side, low, high, y):
    lane, core = lanes()
    for k in range(2):
        place = (lane - 32 * k) & (LANES - 1)
        for f in range(NF):
            with_high = jnp.where(
                (place >= HALF) & (place < HALF + CORNER), high[f], side[f, k]
            )
            y[f, k] = jnp.where(place < CORNER, low[f], with_high)


def units(which):
    return [0.5 / u for u in UNIT] if which else UNIT


def row_maker(which, tile, y, edges, packs):
    lane, core = lanes()
    width = WC if which else WS
    unit = units(which)
    n = width // 2

    def make(i):
        r = i - width
        if 0 <= r < ROWS:
            outer = ((lane + width * (1 - core)) & (LANES - 1)) < width

            def block(f, k):
                shift = LANES - width + width * core - tile_lane(which, r) - 32 * k
                return jnp.where(outer, turn(y[f, k], shift), tile[r, f, k])

        else:
            d = 0 if r < 0 else 1
            away = r - ROWS if d else -1 - r
            j = away if d else i
            w, at = corner(which)[away]
            src, base = packs[d](j % n)
            outer = ((lane + w * (1 - core)) & (LANES - 1)) < w
            inner = ((lane - HALF + w * core) & (LANES - 1)) < w

            def block(f, k):
                v = src[base + 2 * f + k]
                if j >= n:
                    v = turn(v, HALF)
                if w:
                    o = turn(y[f, k], LANES - w + w * core - HALF * d - at - 32 * k)
                    i = turn(edges[d][f], HALF * d - at - 32 * k - w * core)
                    v = jnp.where(inner, i, jnp.where(outer, o, v))
                return v

        return [[block(f, k) * unit[f] for f in range(NF)] for k in range(2)]

    return make


def load(ref, r):
    return [[ref[r, f, k] for f in range(NF)] for k in range(2)]


def invert(x):
    return pltpu.reciprocal(x, approx=True)


STEP = 0.025
UNIT = (1.0, STEP, STEP, STEP, STEP * STEP)
VISC = 0.2 * STEP
KEEP = 1.0 - 6.0 * VISC


def fluxes(v):
    rho, m1, m2, m3, en = v
    inv = invert(rho)
    v1, v2, v3 = m1 * inv, m2 * inv, m3 * inv
    a, b, c = m1 * v1, m2 * v2, m3 * v3
    p = 0.4 * en - 0.2 * (a + b + c)
    h = en + p
    m12, m13, m23 = m1 * v2, m1 * v3, m2 * v3
    return (
        (m1, a + p, m12, m13, h * v1),
        (m2, m12, b + p, m23, h * v2),
        (m3, m13, m23, c + p, h * v3),
    )


def pieces(v, along_y=True):
    before, after, here, left, right = [], [], [], [], []
    fl = [fluxes(v[k]) for k in range(2)]
    for f in range(NF):
        s = [VISC * v[k][f] for k in range(2)]
        before += [s[k] - fl[k][0][f] for k in range(2)]
        after += [s[k] + fl[k][0][f] for k in range(2)]
        if along_y:
            zm = [s[k] - fl[k][2][f] for k in range(2)]
            zp = [s[k] + fl[k][2][f] for k in range(2)]
            here += [
                zm[1] + pltpu.roll(zp[1], 1, 0),
                pltpu.roll(zm[0], 7, 0) + zp[0],
            ]
            left += [s[k] - fl[k][1][f] for k in range(2)]
            right += [s[k] + fl[k][1][f] for k in range(2)]
    return before, after, here, left, right


def rate_pass(get, lo, hi, emit):
    _, after, _, _, _ = pieces(get(lo), False)
    here = left = right = None
    for r in range(lo + 1, hi):
        before, after2, here2, left2, right2 = pieces(get(r), r < hi - 1)
        if here is not None:
            sums = zip(left, right, here, before)
            emit(r - 1, [(turn(a, -1) + turn(b, 1)) + (c + d) for a, b, c, d in sums])
        here = [a + b for a, b in zip(here2, after)]
        after, left, right = after2, left2, right2


def steps(u0, s0, u1, s1, u2):
    def section(base, dst):
        def emit(r, rate):
            for (f, k), x in zip(FK, rate):
                dst[r, f, k] = KEEP * base[r, f, k] + x

        return emit

    def advance(base, sec, dst, shift):
        def emit(r, rate):
            for (f, k), x in zip(FK, rate):
                there = KEEP * sec[r, f, k] + x
                dst[r - shift, f, k] = 0.5 * (base[r, f, k] + there)

        return emit

    def run(ref, emit):
        return lambda lo, hi: rate_pass(lambda r: load(ref, r), lo, hi, emit)

    return (
        run(u0, section(u0, s0)),
        run(s0, advance(u0, s0, u1, 0)),
        run(u1, section(u1, s1)),
        run(s1, advance(u1, s1, u2, WS)),
    )


def outer_forward(u0, s0, u1, s1):
    passes = steps(u0, s0, u1, s1, None)
    for n in range(3):
        passes[n](n, n + 4)
        passes[n](TOTAL - 4 - n, TOTAL - n)


def forward_kernel(
    t0, y, first_low, first_high, rest_low, rest_high, u0, s0, u1, s1, u2
):
    make = row_maker(
        0, t0, y, (first_low, first_high),
        (lambda j: (rest_low, 2 * NF * j), lambda j: (rest_high, 2 * NF * j)),
    )
    for r in range(TOTAL):
        v = make(r)
        for f, k in FK:
            u0[r, f, k] = v[k][f]
    for n, step in enumerate(steps(u0, s0, u1, s1, u2)):
        step(2 + n, TOTAL - 2 - n)

    @pl.when(lax.axis_index("grp") == 1)
    def _():
        outer_forward(u0, s0, u1, s1)


def beside_lanes(row):
    diff, total = [[], []], [[], []]
    for k in range(2):
        for x in row[k]:
            before, after = turn(x, 1), turn(x, -1)
            diff[k].append(after - before)
            total[k].append(after + before)
    return diff, total


def pulled(v, wm, wc, wp, diff, total, emit):
    for k in range(2):
        rho, m1, m2, m3, en = v[k]
        inv = invert(rho)
        v1, v2, v3 = m1 * inv, m2 * inv, m3 * inv
        kin = 0.5 * (v1 * v1 + v2 * v2 + v3 * v3)
        h = 1.4 * (en * inv) - 0.4 * kin
        d1, d2, d3, around = [], diff[k], [], []
        for f in range(NF):
            if k == 0:
                below, above = pltpu.roll(wc[1][f], 1, 0), wc[1][f]
            else:
                below, above = wc[0][f], pltpu.roll(wc[0][f], 7, 0)
            d1.append(wp[k][f] - wm[k][f])
            d3.append(above - below)
            around.append(((wp[k][f] + wm[k][f]) + total[k][f]) + (above + below))
        a = [v1 * d1[f] + v2 * d2[f] + v3 * d3[f] for f in range(1, NF)]
        b1, b2, b3 = [
            d[0] + v1 * d[1] + v2 * d[2] + v3 * d[3] + h * d[4] for d in (d1, d2, d3)
        ]
        pc = 0.4 * (d1[1] + d2[2] + d3[3] + a[3])
        out = [
            pc * kin - (a[0] * v1 + a[1] * v2 + a[2] * v3 + a[3] * h),
            b1 + a[0] - pc * v1,
            b2 + a[1] - pc * v2,
            b3 + a[2] - pc * v3,
            a[3] + pc,
        ]
        for f in range(NF):
            emit(f, k, out[f] + (VISC * around[f] - (6.0 * VISC) * wc[k][f]), wc[k][f])


def pull_pass(state, w, lo, hi, emit, make=None):
    def row(r):
        if make:
            v = make(r)
            for f, k in FK:
                w[r, f, k] = v[k][f]
        return load(w, r)

    row(lo - 1)
    beside = beside_lanes(row(lo))
    for r in range(lo, hi):
        wp = row(r + 1)
        ahead = beside_lanes(wp)
        pulled(
            load(state, r), load(w, r - 1), load(w, r), wp, *beside,
            lambda f, k, x, c: emit(r, f, k, x, c),
        )
        beside = ahead


def send_block(out, i, f, k, lam, state, mine):
    out[i, f, k] = jnp.where(mine, lam, state[i, f, k])


def last_step(s0, u0, lam1, cot, wgt, emit):
    def section(r, f, k, x, w):
        cot[r, f, k] = x
        wgt[r, f, k] = w + x

    def last(r, f, k, x, w):
        emit(r - WS, f, k, lam1[r, f, k] + 0.5 * (cot[r, f, k] + x))

    pull_pass(s0, lam1, 5, TOTAL - 5, section)
    pull_pass(u0, wgt, WS, WS + ROWS, last)


def first_step(s1, u1, lam, cot, wgt, lam1, cuts):
    def section(r, f, k, x, w):
        cot[r, f, k] = x
        wgt[r, f, k] = w + x

    def middle(r, f, k, x, w):
        lam1[r, f, k] = lam[r, f, k] + 0.5 * (cot[r, f, k] + x)

    for lo, hi in cuts[0]:
        pull_pass(s1, lam, lo, hi, section)
    for lo, hi in cuts[1]:
        pull_pass(u1, wgt, lo, hi, middle)


INNER = (((5, TOTAL - 5),), ((6, TOTAL - 6),))
OUTER = (((3, 5), (TOTAL - 5, TOTAL - 3)), ((4, 6), (TOTAL - 6, TOTAL - 4)))


def adjoint_kernel(
    t1, y, first_low, first_high, high, u0, s0, u1, s1, u2,
    lam1, send, lam, cot, wgt, moved,
):
    make = row_maker(
        1, t1, y, (first_low, first_high),
        (
            lambda j: (first_low, NF + 2 * NF * j),
            lambda j: (high, 2 * NF * j),
        ),
    )
    lane, core = lanes()
    mine = owned(lane, core)
    for r in range(2, TOTAL - 2):
        v = make(r - (WS - WC))
        for f, k in FK:
            lam[r, f, k] = v[k][f]
    for i in range(ROWS):
        for f, k in FK:
            away = jnp.where(core == 0, u2[i, f, k], u1[WS + i, f, k])
            moved[i, f, k] = turn(away, HALF)
    first_step(s1, u1, lam, cot, wgt, lam1, INNER)

    @pl.when(core == 0)
    def _():
        for i in range(ROWS):
            for f, k in FK:
                send_block(send, i, f, k, lam1[WS + i, f, k], moved, mine)

    @pl.when(core == 1)
    def _():
        first_step(s1, u1, lam, cot, wgt, lam1, OUTER)
        last_step(
            s0, u0, lam1, cot, wgt,
            lambda i, f, k, x: send_block(send, i, f, k, x, moved, mine),
        )


def finish_kernel(
    a, b, c, d, e, g, u0, lam, u2, keep_a, keep_s, s0, u1, s1, lam1, cot, wgt
):
    core = lax.axis_index("grp")

    @pl.when(core == 0)
    def _():
        def emit(i, f, k, x):
            keep_a[i, f, k] = x
            keep_s[i, f, k] = u1[WS + i, f, k]

        outer_forward(u0, s0, u1, s1)
        first_step(s1, u1, lam, cot, wgt, lam1, OUTER)
        last_step(s0, u0, lam1, cot, wgt, emit)

    @pl.when(core == 1)
    def _():
        for i in range(ROWS):
            for f, k in FK:
                keep_a[i, f, k] = lam1[WS + i, f, k]
                keep_s[i, f, k] = u2[i, f, k]


def merge_kernel(keep_a, keep_s, got, out_a, out_s):
    lane, core = lanes()
    mine = owned(lane, core)
    for f, k in FK:
        for r in range(ROWS):
            rows = pl.ds(f * 16 * ROWS + k * ROWS + r, 8, stride=2 * ROWS)
            other = got[r, f, k]
            out_a[rows, :] = jnp.where(mine, keep_a[r, f, k], other) * (2.0 * UNIT[f])
            there = jnp.where(mine, keep_s[r, f, k], turn(other, HALF))
            out_s[rows, :] = there * (1.0 / UNIT[f])


def call(kernel, name, outs, scratch, *args, flops=0, aliases=None):
    shapes = [jax.ShapeDtypeStruct(s, jnp.float32) for s in outs]
    size = 4 * sum(a.size for a in args)
    return pl.pallas_call(
        kernel,
        out_shape=shapes,
        name=name,
        scratch_shapes=[pltpu.VMEM(s, jnp.float32) for s in scratch],
        input_output_aliases=aliases or {},
        compiler_params=pltpu.CompilerParams(vmem_limit_bytes=VMEM_LIMIT),
        cost_estimate=pl.CostEstimate(flops=flops, bytes_accessed=size, transcendentals=0),
    )(*args)


def rows_of(n):
    return (n, NF, 2, 8, LANES)


def ring(count, step):
    return [(i, (i + step) % count) for i in range(count)]


def shards(endpoints):
    shape = endpoints.shape
    tx, ty = lax.axis_size("tx"), lax.axis_size("ty")
    own = endpoints.reshape(-1, LANES)
    swap = [(0, 1), (1, 0)]
    up, down = ring(tx, 1), ring(tx, -1)
    tile, full = rows_of(ROWS), rows_of(TOTAL)
    block = (NF, 2, 8, LANES)

    def pack(rows):
        return (NF * rows, 8, LANES)

    edge = (NF, 8, LANES)
    got = lax.ppermute(own, "grp", swap)
    (mine,) = call(own_kernel, "own", [tile], [], own, flops=10**6)
    t0, t1, first_up, first_down = call(
        first_kernel, "first", [tile, tile, pack(WC + 1), edge], [], mine, got,
        flops=10**6,
    )
    first_low = lax.ppermute(first_up, "tx", up)
    first_high = lax.ppermute(first_down, "tx", down)
    rest_up, rest_down = call(
        rest_kernel, "rest", [pack(WS), pack(WS)], [], t0, flops=10**6
    )
    (side,) = call(tile_kernel, "tile", [block], [], t0, t1, flops=10**7)
    rest_low = lax.ppermute(rest_up, "tx", up)
    rest_high = lax.ppermute(rest_down, "tx", down)
    (sent,) = call(
        side_kernel, "side", [block], [], side, first_low, first_high, flops=10**10,
    )
    (down1,) = call(late_kernel, "late", [pack(WC)], [], t1, sent, flops=10**6)
    pairs = [(i, ty + (i - 1) % ty) for i in range(ty)]
    pairs += [(b, a) for a, b in pairs]
    y = lax.ppermute(sent, ("grp", "ty"), pairs)
    high1 = lax.ppermute(down1, "tx", down)
    u0, s0, u1, s1, u2 = call(
        forward_kernel, "forward", [full, full, full, full, tile], [],
        t0, y, first_low, first_high, rest_low, rest_high, flops=10**9,
    )
    lam1, send, lam, cot, wgt = call(
        adjoint_kernel, "adjoint", [full, tile, full, full, full], [tile],
        t1, y, first_low, first_high, high1, u0, s0, u1, s1, u2, flops=10**8,
    )
    other = lax.ppermute(send, "grp", swap)
    keep_a, keep_s, *_ = call(
        finish_kernel, "finish", [tile, tile] + [full] * 6, [],
        s0, u1, s1, lam1, cot, wgt, u0, lam, u2,
        flops=10**8, aliases={i: i + 2 for i in range(6)},
    )
    adjoints, states = call(
        merge_kernel, "merge", [own.shape, own.shape], [], keep_a, keep_s, other
    )
    return adjoints.reshape(shape), states.reshape(shape)


def solution(mesh):
    placed = P("grp", None, None, "tx", "ty")
    return jax.shard_map(
        shards, mesh=mesh, in_specs=(placed,), out_specs=(placed, placed), check_vma=False
    )
```

```python
import jax
import jax.numpy as jnp
from jax import lax
from jax.experimental import pallas as pl
from jax.experimental.pallas import tpu as pltpu
from jax.sharding import PartitionSpec as P


NF = 5
WS = 6
WC = 4
ROWS = 8
HALF = 64
LANES = 128
TOTAL = ROWS + 2 * WS
FK = [(f, k) for f in range(NF) for k in range(2)]
VMEM_LIMIT = 32 * 2**20
UP1 = WS * NF
CORNER = WS * (WS - 1) // 2 + WC * (WC - 1) // 2


def lanes():
    lane = lax.broadcasted_iota(jnp.int32, (8, LANES), 1)
    core = lax.axis_index("grp")
    return lane, core


def owned(lane, core):
    return ((lane + HALF * core) & (LANES - 1)) < HALF


def turn(x, shift):
    if isinstance(shift, int):
        shift %= LANES
    else:
        shift &= LANES - 1
    return pltpu.roll(x, shift, 1)


def triangle(width, base):
    return [(w, base + w * (w - 1) // 2) for w in reversed(range(width))]


def corner(which):
    return triangle(WS, 0) if which == 0 else triangle(WC, WS * (WS - 1) // 2)


def tile_lane(which, r):
    if which == 0:
        return CORNER + WS * r if r < 5 else HALF + CORNER + WS * (r - 5)
    if r < 3:
        return CORNER + 5 * WS + WC * r
    return HALF + CORNER + 3 * WS + WC * (r - 3)


def own_kernel(own, rows_out):
    for f, k in FK:
        for r in range(ROWS):
            rows = pl.ds(f * 16 * ROWS + k * ROWS + r, 8, stride=2 * ROWS)
            rows_out[r, f, k] = own[rows, :]


def pack_rows(tile, out, start, n, pairs, base, lane, core):
    mine = owned(lane, core)
    for i, j in enumerate(pairs):
        for f, k in FK:
            other = turn(tile[start + n + j, f, k], HALF)
            at = base + 2 * NF * i + 2 * f + k
            out[at] = jnp.where(mine, tile[start + j, f, k], other)


def first_kernel(own, got, t0, t1, first_up, first_down):
    lane, core = lanes()
    first = core == 0
    zero = jnp.zeros((8, LANES), jnp.float32)
    edges = [[zero] * NF for _ in range(2)]
    for r in range(ROWS):
        rows = [[], []]
        for f, k in FK:
            at = pl.ds(f * 16 * ROWS + k * ROWS + r, 8, stride=2 * ROWS)
            a, b = own[r, f, k], got[at, :]
            rows[0].append(jnp.where(first, a, b))
            rows[1].append(jnp.where(first, b, a))
            t0[r, f, k] = rows[0][-1]
            t1[r, f, k] = rows[1][-1]
        for which, width in ((0, WS), (1, WC)):
            for d, away in ((0, ROWS - 1 - r), (1, r)):
                if away >= width:
                    continue
                w, at = corner(which)[away]
                if w == 0:
                    continue
                for k in range(2):
                    place = (lane - 32 * k) & (HALF - 1)
                    mask = (place >= at) & (place < at + w)
                    for f in range(NF):
                        shift = at + 32 * k + HALF * d + w * core
                        moved = turn(rows[which][2 * f + k], shift)
                        edges[d][f] = jnp.where(mask, moved, edges[d][f])
    for f in range(NF):
        first_up[f] = edges[0][f]
        first_down[f] = edges[1][f]
    pack_rows(t1, first_up, ROWS - WC, WC // 2, (0, 1), NF, lane, core)


def rest_kernel(t0, rest_up, rest_down):
    lane, core = lanes()
    pack_rows(t0, rest_up, ROWS - WS, WS // 2, (0, 1, 2), 0, lane, core)
    pack_rows(t0, rest_down, 0, WS // 2, (0, 1, 2), 0, lane, core)


def late_kernel(t1, y, down1):
    lane, core = lanes()
    pack_rows(t1, down1, 0, WC // 2, (0, 1), 0, lane, core)


def tile_kernel(t0, t1, side):
    lane, core = lanes()
    sides = [jnp.zeros((8, LANES), jnp.float32) for _ in FK]
    for r in range(ROWS):
        for which, width, tile in ((0, WS, t0), (1, WC, t1)):
            at = tile_lane(which, r)
            for k in range(2):
                place = (lane - 32 * k) & (LANES - 1)
                mask = (place >= at) & (place < at + width)
                for f in range(NF):
                    i = 2 * f + k
                    moved = turn(tile[r, f, k], at + 32 * k + width * core)
                    sides[i] = jnp.where(mask, moved, sides[i])
    for i, (f, k) in enumerate(FK):
        side[f, k] = sides[i]


def side_kernel(side, low, high, y):
    lane, core = lanes()
    for k in range(2):
        place = (lane - 32 * k) & (LANES - 1)
        for f in range(NF):
            with_high = jnp.where(
                (place >= HALF) & (place < HALF + CORNER), high[f], side[f, k]
            )
            y[f, k] = jnp.where(place < CORNER, low[f], with_high)


def units(which):
    return [0.5 / u for u in UNIT] if which else UNIT


def row_maker(which, tile, y, edges, packs):
    lane, core = lanes()
    width = WC if which else WS
    unit = units(which)
    n = width // 2

    def make(i):
        r = i - width
        if 0 <= r < ROWS:
            outer = ((lane + width * (1 - core)) & (LANES - 1)) < width

            def block(f, k):
                shift = LANES - width + width * core - tile_lane(which, r) - 32 * k
                return jnp.where(outer, turn(y[f, k], shift), tile[r, f, k])

        else:
            d = 0 if r < 0 else 1
            away = r - ROWS if d else -1 - r
            j = away if d else i
            w, at = corner(which)[away]
            src, base = packs[d](j % n)
            outer = ((lane + w * (1 - core)) & (LANES - 1)) < w
            inner = ((lane - HALF + w * core) & (LANES - 1)) < w

            def block(f, k):
                v = src[base + 2 * f + k]
                if j >= n:
                    v = turn(v, HALF)
                if w:
                    o = turn(y[f, k], LANES - w + w * core - HALF * d - at - 32 * k)
                    i = turn(edges[d][f], HALF * d - at - 32 * k - w * core)
                    v = jnp.where(inner, i, jnp.where(outer, o, v))
                return v

        return [[block(f, k) * unit[f] for f in range(NF)] for k in range(2)]

    return make


def load(ref, r):
    return [[ref[r, f, k] for f in range(NF)] for k in range(2)]


def invert(x):
    return pltpu.reciprocal(x, approx=True)


STEP = 0.025
UNIT = (1.0, STEP, STEP, STEP, STEP * STEP)
VISC = 0.2 * STEP
KEEP = 1.0 - 6.0 * VISC


def fluxes(v):
    rho, m1, m2, m3, en = v
    inv = invert(rho)
    v1, v2, v3 = m1 * inv, m2 * inv, m3 * inv
    a, b, c = m1 * v1, m2 * v2, m3 * v3
    p = 0.4 * en - 0.2 * (a + b + c)
    h = en + p
    m12, m13, m23 = m1 * v2, m1 * v3, m2 * v3
    return (
        (m1, a + p, m12, m13, h * v1),
        (m2, m12, b + p, m23, h * v2),
        (m3, m13, m23, c + p, h * v3),
    )


def pieces(v, along_y=True):
    before, after, here, left, right = [], [], [], [], []
    fl = [fluxes(v[k]) for k in range(2)]
    for f in range(NF):
        s = [VISC * v[k][f] for k in range(2)]
        before += [s[k] - fl[k][0][f] for k in range(2)]
        after += [s[k] + fl[k][0][f] for k in range(2)]
        if along_y:
            zm = [s[k] - fl[k][2][f] for k in range(2)]
            zp = [s[k] + fl[k][2][f] for k in range(2)]
            here += [
                zm[1] + pltpu.roll(zp[1], 1, 0),
                pltpu.roll(zm[0], 7, 0) + zp[0],
            ]
            left += [s[k] - fl[k][1][f] for k in range(2)]
            right += [s[k] + fl[k][1][f] for k in range(2)]
    return before, after, here, left, right


def rate_pass(get, lo, hi, emit):
    _, after, _, _, _ = pieces(get(lo), False)
    here = left = right = None
    for r in range(lo + 1, hi):
        before, after2, here2, left2, right2 = pieces(get(r), r < hi - 1)
        if here is not None:
            sums = zip(left, right, here, before)
            emit(r - 1, [(turn(a, -1) + turn(b, 1)) + (c + d) for a, b, c, d in sums])
        here = [a + b for a, b in zip(here2, after)]
        after, left, right = after2, left2, right2


def steps(u0, s0, u1, s1, u2):
    def section(base, dst):
        def emit(r, rate):
            for (f, k), x in zip(FK, rate):
                dst[r, f, k] = KEEP * base[r, f, k] + x

        return emit

    def advance(base, sec, dst, shift):
        def emit(r, rate):
            for (f, k), x in zip(FK, rate):
                there = KEEP * sec[r, f, k] + x
                dst[r - shift, f, k] = 0.5 * (base[r, f, k] + there)

        return emit

    def run(ref, emit):
        return lambda lo, hi: rate_pass(lambda r: load(ref, r), lo, hi, emit)

    return (
        run(u0, section(u0, s0)),
        run(s0, advance(u0, s0, u1, 0)),
        run(u1, section(u1, s1)),
        run(s1, advance(u1, s1, u2, WS)),
    )


def outer_forward(u0, s0, u1, s1):
    passes = steps(u0, s0, u1, s1, None)
    for n in range(3):
        passes[n](n, n + 4)
        passes[n](TOTAL - 4 - n, TOTAL - n)


def forward_kernel(
    t0, y, first_low, first_high, rest_low, rest_high, u0, s0, u1, s1, u2
):
    make = row_maker(
        0, t0, y, (first_low, first_high),
        (lambda j: (rest_low, 2 * NF * j), lambda j: (rest_high, 2 * NF * j)),
    )
    for r in range(TOTAL):
        v = make(r)
        for f, k in FK:
            u0[r, f, k] = v[k][f]
    for n, step in enumerate(steps(u0, s0, u1, s1, u2)):
        step(2 + n, TOTAL - 2 - n)

    @pl.when(lax.axis_index("grp") == 1)
    def _():
        outer_forward(u0, s0, u1, s1)


def beside_lanes(row):
    diff, total = [[], []], [[], []]
    for k in range(2):
        for x in row[k]:
            before, after = turn(x, 1), turn(x, -1)
            diff[k].append(after - before)
            total[k].append(after + before)
    return diff, total


def pulled(v, wm, wc, wp, diff, total, emit):
    for k in range(2):
        rho, m1, m2, m3, en = v[k]
        inv = invert(rho)
        v1, v2, v3 = m1 * inv, m2 * inv, m3 * inv
        kin = 0.5 * (v1 * v1 + v2 * v2 + v3 * v3)
        h = 1.4 * (en * inv) - 0.4 * kin
        d1, d2, d3, around = [], diff[k], [], []
        for f in range(NF):
            if k == 0:
                below, above = pltpu.roll(wc[1][f], 1, 0), wc[1][f]
            else:
                below, above = wc[0][f], pltpu.roll(wc[0][f], 7, 0)
            d1.append(wp[k][f] - wm[k][f])
            d3.append(above - below)
            around.append(((wp[k][f] + wm[k][f]) + total[k][f]) + (above + below))
        a = [v1 * d1[f] + v2 * d2[f] + v3 * d3[f] for f in range(1, NF)]
        b1, b2, b3 = [
            d[0] + v1 * d[1] + v2 * d[2] + v3 * d[3] + h * d[4] for d in (d1, d2, d3)
        ]
        pc = 0.4 * (d1[1] + d2[2] + d3[3] + a[3])
        out = [
            pc * kin - (a[0] * v1 + a[1] * v2 + a[2] * v3 + a[3] * h),
            b1 + a[0] - pc * v1,
            b2 + a[1] - pc * v2,
            b3 + a[2] - pc * v3,
            a[3] + pc,
        ]
        for f in range(NF):
            emit(f, k, out[f] + (VISC * around[f] - (6.0 * VISC) * wc[k][f]), wc[k][f])


def pull_pass(state, w, lo, hi, emit, make=None):
    def row(r):
        if make:
            v = make(r)
            for f, k in FK:
                w[r, f, k] = v[k][f]
        return load(w, r)

    row(lo - 1)
    beside = beside_lanes(row(lo))
    for r in range(lo, hi):
        wp = row(r + 1)
        ahead = beside_lanes(wp)
        pulled(
            load(state, r), load(w, r - 1), load(w, r), wp, *beside,
            lambda f, k, x, c: emit(r, f, k, x, c),
        )
        beside = ahead


def send_block(out, i, f, k, lam, state, mine):
    out[i, f, k] = jnp.where(mine, lam, turn(state, HALF))


def last_step(s0, u0, lam1, cot, wgt, emit):
    def section(r, f, k, x, w):
        cot[r, f, k] = x
        wgt[r, f, k] = w + x

    def last(r, f, k, x, w):
        emit(r - WS, f, k, lam1[r, f, k] + 0.5 * (cot[r, f, k] + x))

    pull_pass(s0, lam1, 5, TOTAL - 5, section)
    pull_pass(u0, wgt, WS, WS + ROWS, last)


def first_step(s1, u1, lam, cot, wgt, lam1, cuts):
    def section(r, f, k, x, w):
        cot[r, f, k] = x
        wgt[r, f, k] = w + x

    def middle(r, f, k, x, w):
        lam1[r, f, k] = lam[r, f, k] + 0.5 * (cot[r, f, k] + x)

    for lo, hi in cuts[0]:
        pull_pass(s1, lam, lo, hi, section)
    for lo, hi in cuts[1]:
        pull_pass(u1, wgt, lo, hi, middle)


INNER = (((5, TOTAL - 5),), ((6, TOTAL - 6),))
OUTER = (((3, 5), (TOTAL - 5, TOTAL - 3)), ((4, 6), (TOTAL - 6, TOTAL - 4)))


def adjoint_kernel(
    t1, y, first_low, first_high, high, u0, s0, u1, s1, u2,
    lam1, send, lam, cot, wgt,
):
    make = row_maker(
        1, t1, y, (first_low, first_high),
        (
            lambda j: (first_low, NF + 2 * NF * j),
            lambda j: (high, 2 * NF * j),
        ),
    )
    lane, core = lanes()
    mine = owned(lane, core)
    for r in range(2, TOTAL - 2):
        v = make(r - (WS - WC))
        for f, k in FK:
            lam[r, f, k] = v[k][f]
    first_step(s1, u1, lam, cot, wgt, lam1, INNER)

    @pl.when(core == 0)
    def _():
        for i in range(ROWS):
            for f, k in FK:
                send_block(send, i, f, k, lam1[WS + i, f, k], u2[i, f, k], mine)

    @pl.when(core == 1)
    def _():
        first_step(s1, u1, lam, cot, wgt, lam1, OUTER)
        last_step(
            s0, u0, lam1, cot, wgt,
            lambda i, f, k, x: send_block(send, i, f, k, x, u1[WS + i, f, k], mine),
        )


def finish_kernel(
    a, b, c, d, e, g, u0, lam, u2, keep_a, keep_s, s0, u1, s1, lam1, cot, wgt
):
    core = lax.axis_index("grp")

    @pl.when(core == 0)
    def _():
        def emit(i, f, k, x):
            keep_a[i, f, k] = x
            keep_s[i, f, k] = u1[WS + i, f, k]

        outer_forward(u0, s0, u1, s1)
        first_step(s1, u1, lam, cot, wgt, lam1, OUTER)
        last_step(s0, u0, lam1, cot, wgt, emit)

    @pl.when(core == 1)
    def _():
        for i in range(ROWS):
            for f, k in FK:
                keep_a[i, f, k] = lam1[WS + i, f, k]
                keep_s[i, f, k] = u2[i, f, k]


def merge_kernel(keep_a, keep_s, got, out_a, out_s, buf, sem):
    lane, core = lanes()
    mine = owned(lane, core)
    copies = []
    for i, (keep, out) in enumerate(((keep_a, out_a), (keep_s, out_s))):
        for f, k in FK:
            unit = 1.0 / UNIT[f] if i else 2.0 * UNIT[f]
            for r in range(ROWS):
                there = turn(got[r, f, k], HALF) if i else got[r, f, k]
                rows = pl.ds(f * 16 * ROWS + k * ROWS + r, 8, stride=2 * ROWS)
                buf[i, rows, :] = jnp.where(mine, keep[r, f, k], there) * unit
        copies.append(pltpu.make_async_copy(buf.at[i], out, sem.at[i]))
        copies[i].start()
    for copy in copies:
        copy.wait()


def call(kernel, name, outs, scratch, *args, flops=0, aliases=None, **specs):
    shapes = [jax.ShapeDtypeStruct(s, jnp.float32) for s in outs]
    size = 4 * sum(a.size for a in args)
    return pl.pallas_call(
        kernel,
        out_shape=shapes,
        name=name,
        scratch_shapes=[
            pltpu.VMEM(s, jnp.float32) if isinstance(s, tuple) else s for s in scratch
        ],
        input_output_aliases=aliases or {},
        **specs,
        compiler_params=pltpu.CompilerParams(vmem_limit_bytes=VMEM_LIMIT),
        cost_estimate=pl.CostEstimate(flops=flops, bytes_accessed=size, transcendentals=0),
    )(*args)


def rows_of(n):
    return (n, NF, 2, 8, LANES)


def ring(count, step):
    return [(i, (i + step) % count) for i in range(count)]


def shards(endpoints):
    shape = endpoints.shape
    tx, ty = lax.axis_size("tx"), lax.axis_size("ty")
    own = endpoints.reshape(-1, LANES)
    swap = [(0, 1), (1, 0)]
    up, down = ring(tx, 1), ring(tx, -1)
    tile, full = rows_of(ROWS), rows_of(TOTAL)
    block = (NF, 2, 8, LANES)

    def pack(rows):
        return (NF * rows, 8, LANES)

    edge = (NF, 8, LANES)
    got = lax.ppermute(own, "grp", swap)
    (mine,) = call(own_kernel, "own", [tile], [], own, flops=10**6)
    t0, t1, first_up, first_down = call(
        first_kernel, "first", [tile, tile, pack(WC + 1), edge], [], mine, got,
        flops=10**6,
    )
    first_low = lax.ppermute(first_up, "tx", up)
    first_high = lax.ppermute(first_down, "tx", down)
    rest_up, rest_down = call(
        rest_kernel, "rest", [pack(WS), pack(WS)], [], t0, flops=10**6
    )
    (side,) = call(tile_kernel, "tile", [block], [], t0, t1, flops=10**7)
    rest_low = lax.ppermute(rest_up, "tx", up)
    rest_high = lax.ppermute(rest_down, "tx", down)
    (sent,) = call(
        side_kernel, "side", [block], [], side, first_low, first_high, flops=10**10,
    )
    (down1,) = call(late_kernel, "late", [pack(WC)], [], t1, sent, flops=10**6)
    pairs = [(i, ty + (i - 1) % ty) for i in range(ty)]
    pairs += [(b, a) for a, b in pairs]
    y = lax.ppermute(sent, ("grp", "ty"), pairs)
    high1 = lax.ppermute(down1, "tx", down)
    u0, s0, u1, s1, u2 = call(
        forward_kernel, "forward", [full, full, full, full, tile], [],
        t0, y, first_low, first_high, rest_low, rest_high, flops=10**9,
    )
    lam1, send, lam, cot, wgt = call(
        adjoint_kernel, "adjoint", [full, tile, full, full, full], [],
        t1, y, first_low, first_high, high1, u0, s0, u1, s1, u2, flops=10**8,
    )
    other = lax.ppermute(send, "grp", swap)
    keep_a, keep_s, *_ = call(
        finish_kernel, "finish", [tile, tile] + [full] * 6, [],
        s0, u1, s1, lam1, cot, wgt, u0, lam, u2,
        flops=10**8, aliases={i: i + 2 for i in range(6)},
    )
    adjoints, states = call(
        merge_kernel, "merge", [own.shape, own.shape],
        [(2,) + own.shape, pltpu.SemaphoreType.DMA((2,))],
        keep_a, keep_s, other, out_specs=[pl.BlockSpec(memory_space=pl.ANY)] * 2,
    )
    return adjoints.reshape(shape), states.reshape(shape)


def solution(mesh):
    placed = P("grp", None, None, "tx", "ty")
    return jax.shard_map(
        shards, mesh=mesh, in_specs=(placed,), out_specs=(placed, placed), check_vma=False
    )
```
